512 devices in a mesh: gx: 32 (over x, y, core), gy: 16 (over z).
Axes of the slice: x: 4, y: 4, z: 16, core: 2. Of those that a mesh axis runs over, the one named last changes fastest.
Arguments:
- positions: float32 [3, 32, 16, 128], P(None, 'gx', 'gy'), may hold values from 0 to 384, as said below
- neighbours: int32 [32, 32, 16, 128], P(None, 'gx', 'gy'), may hold values from 0 to 1151, as said below
- live_count: int32 [32, 16], P('gx', 'gy'), may hold values from 16 to 128, as said below
- stencil_base: int32 [3, 32, 16, 128], P(None, 'gx', 'gy'), may hold values from -1 to 383, as said below
- spline_weight: float32 [3, 4, 32, 16, 128], P(None, None, 'gx', 'gy'), may hold values from 0 to 1, as said below
- spline_slope: float32 [3, 4, 32, 16, 128], P(None, None, 'gx', 'gy'), may hold values from -1 to 1, as said below
- embed_scale: float32 [100], replicated, may hold values from -12 to 12
- embed_bias: float32 [100], replicated, may hold values from -4 to 4
- desc_gain: float32 [1600], replicated, may hold values from 0.25 to 1.75
- fit_in: bfloat16 [128, 1600], replicated, may hold values from -0.15625 to 0.15625
- fit_bias: float32 [128], replicated, may hold values from -3 to 3
- fit_hidden: bfloat16 [128, 128], replicated, may hold values from -0.5 to 0.5
- fit_bias_two: float32 [128], replicated, may hold values from -3 to 3
- fit_out: float32 [128], replicated, may hold values from -0.5 to 0.5
Outputs:
- centroid_energy: float32 [32, 16, 128], P('gx', 'gy')
- centroid_force: float32 [3, 32, 16, 128], P(None, 'gx', 'gy')
The draws below stay inside these ranges and needn't reach their ends.
Inputs may be any that keep to these rules, and one draw needn't show every extreme that they name: `live_count`: slots below a column's count are live; some column has all 128 slots live. `neighbours`: every entry names a live slot of one of the nine blocks of the column's neighbourhood. `stencil_base`: along x the base lies in -1 to 10, along y in -1 to 22, along z in 0 to 383. `positions`: x lies in 0 to 12, y in 0 to 24, z in 0 to 384. `spline_weight`: cubic B-spline weights of a fraction in [0, 1) for each axis; the four weights sum to one. `spline_slope`: the derivatives of those weights with respect to the fraction.
All inputs are finite; a program needn't handle non-finite values.
Results may differ from the reference program's by a relative error of at most 0.006.
The reference program's roundings to bfloat16 on the way (of `normed`) count: a program that leaves them out, or rounds other values in their place, can miss the bound.
Values sent between devices are 32-bit elements; how exact they have to be, the bound alone decides.
No kernel may reach another device: no remote copies, remote signals or barrier semaphores. Data moves between devices by JAX's collectives and lax.ppermute only.
A program may use at most 64 MiB of HBM per device.

```python
import math
import jax
import jax.numpy as jnp
from jax import lax

GRID = 384
EMB = 100
AXIS = 16
FIT = 128
NEIGH = 32
ATOM_DEV = 128
DESC = 1600
CX = 12
CY = 24
N_GX = 32
N_GY = 16


def live_counts(key):
    fewest = ATOM_DEV // 8
    spread_range = ATOM_DEV - fewest
    picked = jax.random.randint(jax.random.fold_in(key, 101), (N_GX, N_GY), 0, spread_range + 1)
    counts = fewest + picked * picked // spread_range
    fullest = jax.random.randint(jax.random.fold_in(key, 102), (), 0, N_GX * N_GY)
    flat = jnp.where(jnp.arange(N_GX * N_GY) == fullest, ATOM_DEV, counts.reshape(-1))
    return flat.reshape(N_GX, N_GY).astype(jnp.int32)


def draw_live_count(key, part):
    return live_counts(key)


def draw_neighbours(key, part):
    counts = live_counts(key)
    shape = (NEIGH, N_GX, N_GY, ATOM_DEV)
    block = jax.random.randint(jax.random.fold_in(key, 103), shape, 0, 9)
    stride_x = block // 3 - 1
    stride_y = block % 3 - 1
    rows = lax.broadcasted_iota(jnp.int32, shape, 1)
    cols = lax.broadcasted_iota(jnp.int32, shape, 2)
    slots = lax.broadcasted_iota(jnp.int32, shape, 3)
    other = counts[(rows + stride_x) % N_GX, (cols + stride_y) % N_GY]
    owned = counts[rows, cols]
    aligned = jnp.minimum(slots, owned - 1) * other // owned
    jitter = jax.random.randint(jax.random.fold_in(key, 104), shape, -3, 4)
    chosen = jnp.clip(aligned + jitter, 0, other - 1)
    return (block * ATOM_DEV + chosen).astype(jnp.int32)


def draw_positions(key, part):
    counts = live_counts(key)
    shape = (N_GX, N_GY, ATOM_DEV)
    fraction = jax.random.uniform(jax.random.fold_in(key, 105), (3,) + shape, jnp.float32)
    slots = lax.broadcasted_iota(jnp.int32, shape, 2)
    owned = counts[:, :, None]
    height = jnp.where(slots < owned, (slots.astype(jnp.float32) + fraction[2]) / owned.astype(jnp.float32), fraction[2])
    coord_x = fraction[0] * (GRID // N_GX)
    coord_y = fraction[1] * (GRID // N_GY)
    coord_z = jnp.minimum(height * GRID, GRID * 0.999)
    return jnp.stack([coord_x, coord_y, coord_z]).astype(jnp.float32)


def draw_stencil_base(key, part):
    shape = (N_GX, N_GY, ATOM_DEV)
    base_x = jax.random.randint(jax.random.fold_in(key, 107), shape, -1, GRID // N_GX - 1)
    base_y = jax.random.randint(jax.random.fold_in(key, 108), shape, -1, GRID // N_GY - 1)
    base_z = jax.random.randint(jax.random.fold_in(key, 109), shape, 0, GRID)
    return jnp.stack([base_x, base_y, base_z]).astype(jnp.int32)


def spline_fraction(key):
    fraction = jax.random.uniform(jax.random.fold_in(key, 106), (3, N_GX, N_GY, ATOM_DEV), jnp.float32)
    return fraction


def draw_spline_weight(key, part):
    fraction = spline_fraction(key)
    remain = 1.0 - fraction
    cube = fraction * fraction * fraction
    square = fraction * fraction
    values = [remain * remain * remain / 6.0, (3.0 * cube - 6.0 * square + 4.0) / 6.0, (-3.0 * cube + 3.0 * square + 3.0 * fraction + 1.0) / 6.0, cube / 6.0]
    return jnp.stack(values, axis=1).astype(jnp.float32)


def draw_spline_slope(key, part):
    fraction = spline_fraction(key)
    remain = 1.0 - fraction
    square = fraction * fraction
    values = [-0.5 * remain * remain, (3.0 * square - 4.0 * fraction) / 2.0, (-3.0 * square + 2.0 * fraction + 1.0) / 2.0, 0.5 * square]
    return jnp.stack(values, axis=1).astype(jnp.float32)


def normal_values(stream_key, shape, spread, limit, kind=jnp.bfloat16):
    values = jax.random.normal(stream_key, shape, jnp.float32) * spread
    return jnp.minimum(jnp.maximum(values, -limit), limit).astype(kind)


def setup_inputs(seed: int = 0) -> dict:
    keys = jax.random.split(jax.random.key(seed), 15)
    return {
        "positions": draw_positions(jax.random.fold_in(keys[14], 71), 0),
        "neighbours": draw_neighbours(jax.random.fold_in(keys[14], 71), 0),
        "live_count": draw_live_count(jax.random.fold_in(keys[14], 71), 0),
        "stencil_base": draw_stencil_base(jax.random.fold_in(keys[14], 71), 0),
        "spline_weight": draw_spline_weight(jax.random.fold_in(keys[14], 71), 0),
        "spline_slope": draw_spline_slope(jax.random.fold_in(keys[14], 71), 0),
        "embed_scale": normal_values(keys[6], (EMB,), 3.0, 12.0, jnp.float32),
        "embed_bias": normal_values(keys[7], (EMB,), 1.0, 4.0, jnp.float32),
        "desc_gain": jnp.clip(1.0 + 0.15 * jax.random.normal(keys[8], (DESC,), jnp.float32), 0.25, 1.75),
        "fit_in": normal_values(keys[9], (FIT, DESC), DESC ** -0.5, 0.15625),
        "fit_bias": normal_values(keys[10], (FIT,), 0.5, 3.0, jnp.float32),
        "fit_hidden": normal_values(keys[11], (FIT, FIT), FIT ** -0.5, 0.5),
        "fit_bias_two": normal_values(keys[12], (FIT,), 0.5, 3.0, jnp.float32),
        "fit_out": normal_values(keys[13], (FIT,), FIT ** -0.5, 0.5, jnp.float32),
    }


highest = lax.Precision.HIGHEST
radius_scale = 4.0
screen_width = 0.25
norm_floor = 1e-06
full_turn = 2.0 * math.pi

def stencil_table(anchor, weights, length, offset, periodic):
    count = anchor.shape[0]
    cell_index = lax.broadcasted_iota(jnp.int32, (4, length, count), 1)
    tap_index = lax.broadcasted_iota(jnp.int32, (4, length, count), 0)
    target = anchor[None, None, :] + tap_index + offset
    if periodic:
        target = target % length
    chosen = jnp.where(target == cell_index, weights[:, None, :], jnp.zeros((), weights.dtype))
    return lax.optimization_barrier(jnp.sum(chosen, axis=0))

def spread_cells(charge, anchor, weights, extent_x, extent_y, offset, length):
    table_x = stencil_table(anchor[0], weights[0] * charge[None, :], extent_x, offset, False)
    table_y = stencil_table(anchor[1], weights[1], extent_y, offset, False)
    table_z = stencil_table(anchor[2], weights[2], length, 0, True)
    planes = (table_x[:, None, :] * table_y[None, :, :]).reshape(extent_x * extent_y, -1)
    return jnp.dot(planes, table_z.T, precision=highest).reshape(extent_x, extent_y, length)

def interpolate(padded, anchor, weights, slopes):
    extent_x, extent_y, length = padded.shape
    table_x = stencil_table(anchor[0], weights[0], extent_x, 2, False)
    slope_x = stencil_table(anchor[0], slopes[0], extent_x, 2, False)
    table_y = stencil_table(anchor[1], weights[1], extent_y, 2, False)
    slope_y = stencil_table(anchor[1], slopes[1], extent_y, 2, False)
    table_z = stencil_table(anchor[2], weights[2], length, 0, True)
    slope_z = stencil_table(anchor[2], slopes[2], length, 0, True)
    flat = padded.reshape(extent_x * extent_y, length)
    along = jnp.dot(flat, table_z, precision=highest).reshape(extent_x, extent_y, -1)
    slant = jnp.dot(flat, slope_z, precision=highest).reshape(extent_x, extent_y, -1)
    over_y = lax.optimization_barrier(jnp.sum(along * table_y[None], axis=1))
    value = lax.optimization_barrier(jnp.sum(table_x * over_y, axis=0))
    field_x = -lax.optimization_barrier(jnp.sum(slope_x * over_y, axis=0))
    over_x = lax.optimization_barrier(jnp.sum(along * table_x[:, None, :], axis=0))
    field_y = -lax.optimization_barrier(jnp.sum(slope_y * over_x, axis=0))
    slant_y = lax.optimization_barrier(jnp.sum(slant * table_y[None], axis=1))
    field_z = -lax.optimization_barrier(jnp.sum(table_x * slant_y, axis=0))
    return (value, jnp.stack([field_x, field_y, field_z]))

def fitted_charge(nearby, listed, count, embed_scale, embed_bias, desc_gain, fit_in, fit_bias, fit_hidden, fit_bias_two, fit_out):
    atoms = listed.shape[1]
    center = nearby[:, 4 * atoms:5 * atoms]
    picked = jnp.take(nearby, listed.reshape(-1), axis=1).reshape(3, listed.shape[0], atoms)
    delta = picked - center[:, None, :]
    radius = jnp.sqrt(lax.optimization_barrier(jnp.sum(delta * delta, axis=0)))
    smooth = 1.0 / (1.0 + radius / radius_scale)
    factor = smooth / (radius + radius_scale)
    envelope = jnp.concatenate([smooth[None], delta * factor[None]], axis=0)
    embed = jnp.tanh(smooth[None] * embed_scale[:, None, None] + embed_bias[:, None, None])
    mixed = jnp.einsum('ekn,ckn->ecn', embed, envelope, precision=highest)
    descriptor = jnp.einsum('ecn,acn->ean', mixed, mixed[:AXIS], precision=highest).reshape(-1, atoms)
    scaling = lax.rsqrt(lax.optimization_barrier(jnp.mean(descriptor * descriptor, axis=0)) + norm_floor)
    normed = (descriptor * scaling[None, :] * desc_gain[:, None]).astype(jnp.bfloat16)
    first = jnp.tanh(jnp.dot(fit_in, normed, preferred_element_type=jnp.float32) + fit_bias[:, None])
    second = jnp.tanh(jnp.dot(fit_hidden, first.astype(jnp.bfloat16), preferred_element_type=jnp.float32) + fit_bias_two[:, None]) + first
    charge = lax.optimization_barrier(jnp.sum(fit_out[:, None] * second, axis=0))
    slot_index = lax.broadcasted_iota(jnp.int32, (atoms,), 0)
    return jnp.where(slot_index < count, charge, jnp.zeros((), charge.dtype))

def wave_number(index, length):
    signed = jnp.where(index > length // 2, index - length, index)
    return signed.astype(jnp.float32) * (full_turn / length)

def green_values(index_x, index_y, index_z, length):
    wave_x = wave_number(index_x, length)
    wave_y = wave_number(index_y, length)
    wave_z = wave_number(index_z, length)
    square = wave_x * wave_x + wave_y * wave_y + wave_z * wave_z
    safe = jnp.where(square > 0, square, 1.0)
    value = 2.0 * full_turn * jnp.exp(-0.5 * screen_width * screen_width * square) / safe
    keep = (square > 0) & (index_z != length // 2)
    return jnp.where(keep, value, 0.0)

def fold_edges(padded, length):
    inner = padded[2:length + 2]
    inner = inner.at[0:2].add(padded[length + 2:length + 4])
    inner = inner.at[length - 2:length].add(padded[0:2])
    return inner

def reference(positions, neighbours, live_count, stencil_base, spline_weight, spline_slope, embed_scale, embed_bias, desc_gain, fit_in, fit_bias, fit_hidden, fit_bias_two, fit_out):
    blocks = []
    for stride_x in (-1, 0, 1):
        for stride_y in (-1, 0, 1):
            moved = jnp.roll(positions, (-stride_x, -stride_y), axis=(1, 2))
            offset = jnp.array([stride_x * CX, stride_y * CY, 0], dtype=positions.dtype)
            blocks.append(moved + offset[:, None, None, None])
    stacked = jnp.stack(blocks, axis=1)
    nearby = jnp.transpose(stacked, (2, 3, 0, 1, 4)).reshape(N_GX, N_GY, 3, 9 * ATOM_DEV)
    listed = jnp.transpose(neighbours, (1, 2, 0, 3))

    def one_column(nearby_one, listed_one, count_one):
        return fitted_charge(nearby_one, listed_one, count_one, embed_scale, embed_bias, desc_gain, fit_in, fit_bias, fit_hidden, fit_bias_two, fit_out)

    def one_row(items):
        return jax.vmap(one_column)(items[0], items[1], items[2])
    charges = lax.map(one_row, (nearby, listed, live_count))
    anchors = jnp.transpose(stencil_base, (1, 2, 0, 3))
    weights = jnp.transpose(spline_weight, (2, 3, 0, 1, 4))
    slopes = jnp.transpose(spline_slope, (2, 3, 0, 1, 4))

    def place(index, grid):
        row_index = (index // N_GY).astype(jnp.int32)
        col_index = (index % N_GY).astype(jnp.int32)
        cells = spread_cells(charges[row_index, col_index], anchors[row_index, col_index], weights[row_index, col_index], CX + 4, CY + 4, 2, GRID)
        start = (row_index * CX, col_index * CY, jnp.zeros((), jnp.int32))
        before = lax.dynamic_slice(grid, start, cells.shape)
        return lax.dynamic_update_slice(grid, before + cells, start)
    grid = lax.fori_loop(0, N_GX * N_GY, place, jnp.zeros((GRID + 4, GRID + 4, GRID), jnp.float32))
    grid = fold_edges(grid, GRID)
    density = jnp.swapaxes(fold_edges(jnp.swapaxes(grid, 0, 1), GRID), 0, 1)
    modes = jnp.arange(GRID, dtype=jnp.int32)
    green = green_values(modes[:, None, None], modes[None, :, None], modes[None, None, :], GRID)
    spectrum = jnp.fft.fftn(density) * green
    potential = jnp.real(jnp.fft.ifftn(spectrum)).astype(jnp.float32)
    padded = jnp.pad(potential, ((2, 2), (2, 2), (0, 0)), mode='wrap')

    def gather_one(index):
        row_index = (index // N_GY).astype(jnp.int32)
        col_index = (index % N_GY).astype(jnp.int32)
        start = (row_index * CX, col_index * CY, jnp.zeros((), jnp.int32))
        window = lax.dynamic_slice(padded, start, (CX + 4, CY + 4, GRID))
        value, field = interpolate(window, anchors[row_index, col_index], weights[row_index, col_index], slopes[row_index, col_index])
        charge = charges[row_index, col_index]
        return (0.5 * charge * value, charge[None, :] * field)
    energy, force = lax.map(gather_one, jnp.arange(N_GX * N_GY, dtype=jnp.int32))
    energy = energy.reshape(N_GX, N_GY, ATOM_DEV)
    force = jnp.transpose(force.reshape(N_GX, N_GY, 3, ATOM_DEV), (2, 0, 1, 3))
    return (energy, force)
```

```python
import math

import jax
import jax.numpy as jnp
import numpy as np
from jax import lax
from jax.experimental import pallas as pl
from jax.experimental.pallas import tpu as pltpu
from jax.sharding import PartitionSpec as P

GRID = 384
AXIS = 16
ATOMS = 128
NEIGH = 32
EMB = 100
EMB_ROWS = 104
DESC = 1600
CX = 12
CY = 24
N_GX = 32
N_GY = 16
SLOTS = 24
LANES = 96
WIN = 256
HALF = 1024

radius_scale = 4.0
screen_width = 0.25
norm_floor = 1e-06
full_turn = 2.0 * math.pi
f32 = jnp.float32
bf16 = jnp.bfloat16


def axis_modes():
    freq = np.concatenate([np.arange(193), np.arange(1, 192)])
    is_sine = np.concatenate([np.zeros(193), np.ones(191)]).astype(np.int64)
    return freq, is_sine


def mode_table(cells):
    freq, is_sine = axis_modes()
    turn = (freq[:, None] * cells[None, :] - 96 * is_sine[:, None]) % GRID
    return np.cos(full_turn * turn / GRID)


def mode_weight(freq):
    return np.where((freq == 0) | (freq == GRID // 2), 1.0, 2.0) / GRID


def halves(table):
    table = table.astype(np.float32)
    upper = table.astype(jnp.bfloat16)
    lower = (table - upper.astype(np.float32)).astype(jnp.bfloat16)
    return upper, lower


FREQ, _ = axis_modes()
WAVE = full_turn / GRID
CELLS_X = (np.arange(N_GX)[:, None] * CX + np.arange(16)[None, :] - 1).reshape(-1) % GRID
CELLS_Y = (np.arange(2)[:, None] * 8 * CY + np.arange(WIN)[None, :] - 1).reshape(-1) % GRID
TABLE_X = mode_table(CELLS_X)
TABLE_Y = mode_table(CELLS_Y)
X_IN = halves(TABLE_X)
X_OUT = halves(TABLE_X.T)
Y_IN = halves(TABLE_Y.T)
Y_OUT = halves(TABLE_Y)
SQUARE_X = np.broadcast_to(((FREQ * WAVE) ** 2)[:, None], (GRID, 128)).astype(np.float32)
WEIGHT_X = np.broadcast_to(mode_weight(FREQ)[:, None], (GRID, 128)).astype(np.float32)
SQUARE_Y = np.zeros((4, 1, 128), np.float32)
SQUARE_Y[:, 0, :LANES] = ((FREQ * WAVE) ** 2).reshape(4, LANES)
WEIGHT_Y = np.zeros((4, 1, 128), np.float32)
WEIGHT_Y[:, 0, :LANES] = mode_weight(FREQ).reshape(4, LANES)


def split(value):
    upper = value.astype(bf16)
    return upper, (value - upper.astype(f32)).astype(bf16)


def product(left, right, dims=(((1,), (0,)), ((), ()))):
    a, b = left
    c, d = right
    dot = lambda x, y: lax.dot_general(x, y, dims, preferred_element_type=f32)
    return dot(a, c) + (dot(a, d) + dot(b, c))


def vmem(count):
    return [pl.BlockSpec(memory_space=pltpu.VMEM)] * count


SMEM = pl.BlockSpec(memory_space=pltpu.SMEM)
PARAMS = pltpu.CompilerParams(vmem_limit_bytes=48 * 1024 * 1024)


def charge_kernel(
    count, before, middle, after, listed, base, weight, packed, gain, fit_in, fit_hidden,
    sites, own, mixed, descriptor, normed,
):
    entry = listed[...]
    block = lax.shift_right_logical(entry, 7)
    slot = jnp.bitwise_and(entry, ATOMS - 1)
    picked = [jnp.zeros((NEIGH, ATOMS), f32) for _ in range(3)]
    for a, rows in enumerate((before, middle, after)):
        for b in range(3):
            here = block == a * 3 + b
            for c, shift in enumerate(((a - 1) * CX, (b - 1) * CY, 0)):
                row = rows[b * 3 + c : b * 3 + c + 1, :] + float(shift)
                row = jnp.broadcast_to(row, (NEIGH, ATOMS))
                value = jnp.take_along_axis(row, slot, axis=1)
                picked[c] = jnp.where(here, value, picked[c])
    delta = [picked[c] - middle[3 + c : 4 + c, :] for c in range(3)]
    radius = jnp.sqrt(delta[0] * delta[0] + delta[1] * delta[1] + delta[2] * delta[2])
    smooth = 1.0 / (1.0 + radius / radius_scale)
    factor = smooth / (radius + radius_scale)
    envelope = [smooth] + [d * factor for d in delta]

    columns = jnp.transpose(packed[...])
    column = lambda k, lo, hi: jnp.broadcast_to(columns[lo:hi, k : k + 1], (hi - lo, ATOMS))
    for lo, hi in ((0, 32), (32, 64), (64, EMB_ROWS)):
        scale, bias = column(0, lo, hi), column(1, lo, hi)
        total = [jnp.zeros((hi - lo, ATOMS), f32) for _ in range(4)]
        for k in range(NEIGH):
            embed = jnp.tanh(smooth[k : k + 1, :] * scale + bias)
            for c in range(4):
                total[c] = total[c] + embed * envelope[c][k : k + 1, :]
        for c in range(4):
            mixed[c, lo:hi, :] = total[c]
    second_factor = [mixed[c, 0:AXIS, :] for c in range(4)]
    squares = jnp.zeros((AXIS, ATOMS), f32)
    for e in range(EMB):
        value = mixed[0, e : e + 1, :] * second_factor[0]
        for c in range(1, 4):
            value = value + mixed[c, e : e + 1, :] * second_factor[c]
        squares = squares + value * value
        descriptor[e * AXIS : (e + 1) * AXIS, :] = value
    mean = jnp.sum(squares, axis=0, keepdims=True) * (1.0 / DESC)
    scaling = lax.rsqrt(mean + norm_floor)
    for e in range(EMB):
        rows = slice(e * AXIS, (e + 1) * AXIS)
        value = descriptor[rows, :] * scaling * jnp.broadcast_to(gain[rows, :], (AXIS, ATOMS))
        normed[rows, :] = value.astype(bf16)
    first = jnp.tanh(
        jnp.dot(fit_in[...], normed[...], preferred_element_type=f32) + column(2, 0, 128)
    )
    second = (
        jnp.tanh(
            jnp.dot(fit_hidden[...], first.astype(bf16), preferred_element_type=f32)
            + column(3, 0, 128)
        )
        + first
    )
    charge = jnp.sum(column(4, 0, 128) * second, axis=0, keepdims=True)
    place = lax.broadcasted_iota(jnp.int32, (1, ATOMS), 1)
    charge = jnp.where(place < count[0, 0], charge, 0.0)
    own[...] = charge
    fraction = weight[1] + 2.0 * weight[2] + 3.0 * weight[3] - 1.0
    record = jnp.concatenate(
        [base[...].astype(f32), fraction, charge, jnp.zeros((1, ATOMS), f32)], axis=0
    )
    for j in range(N_GY):
        sites[j] = record


def spline(fraction):
    remain = 1.0 - fraction
    square = fraction * fraction
    cube = square * fraction
    return [
        remain * remain * remain * (1.0 / 6.0),
        (3.0 * cube - 6.0 * square + 4.0) * (1.0 / 6.0),
        (-3.0 * cube + 3.0 * square + 3.0 * fraction + 1.0) * (1.0 / 6.0),
        cube * (1.0 / 6.0),
    ]


def spline_rate(fraction):
    remain = 1.0 - fraction
    square = fraction * fraction
    return [
        -0.5 * remain * remain,
        (3.0 * square - 4.0 * fraction) * 0.5,
        (-3.0 * square + 2.0 * fraction + 1.0) * 0.5,
        0.5 * square,
    ]


def tap_table(first, values, rows):
    away = lax.broadcasted_iota(jnp.int32, (rows, ATOMS), 0).astype(f32) - first
    total = jnp.zeros((rows, ATOMS), f32)
    for t, value in enumerate(values):
        total = jnp.where(away == float(t), value, total)
    return total


def cos_sin(step):
    step = step - GRID * jnp.round(step * (1.0 / GRID))
    quarter = jnp.round(step * (1.0 / 96.0))
    angle = (step - 96.0 * quarter) * WAVE
    square = angle * angle
    sine = angle * (
        1.0 + square * (-1.0 / 6 + square * (1.0 / 120 + square * (-1.0 / 5040 + square / 362880)))
    )
    cosine = 1.0 + square * (
        -0.5 + square * (1.0 / 24 + square * (-1.0 / 720 + square * (1.0 / 40320 - square / 3628800)))
    )
    odd = jnp.abs(quarter) == 1.0
    straight = jnp.where(jnp.abs(quarter) == 2.0, -1.0, 1.0)
    turned = jnp.where(odd, quarter, straight)
    cos_value = jnp.where(odd, -sine, cosine) * turned
    sin_value = jnp.where(odd, cosine, sine) * turned
    return cos_value, sin_value


def z_setup(device):
    row = lax.broadcasted_iota(jnp.int32, (SLOTS, ATOMS), 0)
    is_sine = row >= 12
    freq = (device * 12 + jnp.where(is_sine, row - 12, row)).astype(f32)
    phase = jnp.where(is_sine, 96.0, 0.0)
    turns = [cos_sin(freq * float(t)) for t in range(4)]
    return freq, phase, turns


def z_modes(setup, base, lists):
    freq, phase, turns = setup
    cosine, sine = cos_sin(freq * base - phase)
    out = []
    for values in lists:
        along = values[0] + sum(values[t] * turns[t][0] for t in range(1, 4))
        across = sum(values[t] * turns[t][1] for t in range(1, 4))
        out.append(cosine * along - sine * across)
    return out


def window(j):
    offset = CY * (j % 8)
    start = offset // 16 * 16
    return start, offset - start


def forward_kernel(device, sites, y_hi, y_lo, out, u_hi, u_lo, w_hi, w_lo, packed):
    setup = z_setup(device[0])
    w_hi[...] = jnp.zeros(w_hi.shape, bf16)
    w_lo[...] = jnp.zeros(w_lo.shape, bf16)
    total = None
    for half in range(2):
        for c in range(8):
            j = half * 8 + c
            lanes = slice(c * ATOMS, (c + 1) * ATOMS)
            row = lambda r: sites[j, r : r + 1, :]
            weight_x = [w * row(6) for w in spline(row(3))]
            table_x = tap_table(row(0) + 1.0, weight_x, 16)
            start, shift = window(j)
            table_y = tap_table(row(1) + (1.0 + shift), spline(row(4)), 48)
            hi, lo = split(table_y)
            w_hi[half, start : start + 48, lanes] = hi
            w_lo[half, start : start + 48, lanes] = lo
            (along_z,) = z_modes(setup, row(2), [spline(row(5))])
            for m in range(SLOTS):
                hi, lo = split(along_z[m : m + 1, :] * table_x)
                u_hi[half, m * 16 : (m + 1) * 16, lanes] = hi
                u_lo[half, m * 16 : (m + 1) * 16, lanes] = lo
        cells = product(
            (u_hi[half], u_lo[half]), (w_hi[half], w_lo[half]), (((1,), (1,)), ((), ()))
        )
        rows = slice(half * WIN, (half + 1) * WIN)
        part = product(split(cells), (y_hi[rows, :], y_lo[rows, :]))
        total = part if total is None else total + part
    packed[...] = total
    for kq in range(4):
        block = packed[:, kq * LANES : (kq + 1) * LANES]
        for sg in range(8):
            out[sg * 4 + kq, :, 0:LANES] = block[sg * 48 : sg * 48 + 36, :]
            for p in range(3):
                out[sg * 4 + kq, 12 * p : 12 * p + 12, LANES:128] = block[
                    sg * 48 + 36 : sg * 48 + 48, 32 * p : 32 * p + 32
                ]


def x_kernel(square, weight, sx, wx, in_hi, in_lo, out_hi, out_lo, got, out, held):
    for i in range(N_GX):
        rows = slice(i * 16, (i + 1) * 16)
        for q in range(2):
            held[rows, q * 128 : q * 128 + LANES] = got[i, 16 * q : 16 * q + 16, 0:LANES]
        lane = 2 * 128
        held[i * 16 : i * 16 + 4, lane : lane + LANES] = got[i, 32:36, 0:LANES]
        for p in range(3):
            held[i * 16 + 4 : i * 16 + 16, lane + 32 * p : lane + 32 * p + 32] = got[
                i, 12 * p : 12 * p + 12, LANES:128
            ]
    result = []
    for q in range(3):
        lanes = slice(q * 128, q * 128 + 128)
        place = lax.broadcasted_iota(jnp.int32, (N_GX * 16, 128), 1)
        cells = jnp.where(place < LANES, held[:, lanes], 0.0)
        modes = product((in_hi[...], in_lo[...]), split(cells))
        wave = sx[...] + square[q : q + 1, :]
        safe = jnp.where(wave > 0, wave, 1.0)
        green = 2.0 * full_turn * jnp.exp(-0.5 * screen_width * screen_width * wave) / safe
        green = jnp.where(wave > 0, green, 0.0)
        modes = modes * (green * (wx[...] * weight[q : q + 1, :]))
        result.append(product((out_hi[...], out_lo[...]), split(modes)))
    for q in range(3):
        held[:, q * 128 : q * 128 + 128] = result[q]
    for i in range(N_GX):
        rows = slice(i * 16, (i + 1) * 16)
        for q in range(2):
            out[i, 16 * q : 16 * q + 16, 0:LANES] = held[rows, q * 128 : q * 128 + LANES]
        lane = 2 * 128
        out[i, 32:36, 0:LANES] = held[i * 16 : i * 16 + 4, lane : lane + LANES]
        for p in range(3):
            out[i, 12 * p : 12 * p + 12, LANES:128] = held[
                i * 16 + 4 : i * 16 + 16, lane + 32 * p : lane + 32 * p + 32
            ]


def inverse_kernel(device, sites, y_hi, y_lo, got, out, modes, w_hi, w_lo, d_hi, d_lo, field, rate):
    setup = z_setup(device[0])
    for kq in range(4):
        lanes = slice(kq * LANES, (kq + 1) * LANES)
        for sg in range(8):
            row = sg * 48
            modes[row : row + 36, lanes] = got[sg * 4 + kq, :, 0:LANES]
            for p in range(3):
                modes[row + 36 : row + 48, kq * LANES + 32 * p : kq * LANES + 32 * p + 32] = got[
                    sg * 4 + kq, 12 * p : 12 * p + 12, LANES:128
                ]
    spectrum = split(modes[...])
    for ref in (w_hi, w_lo, d_hi, d_lo):
        ref[...] = jnp.zeros(ref.shape, bf16)
    for half in range(2):
        for c in range(8):
            j = half * 8 + c
            lanes = slice(c * ATOMS, (c + 1) * ATOMS)
            start, shift = window(j)
            first = sites[j, 1:2, :] + (1.0 + shift)
            fraction = sites[j, 4:5, :]
            for values, hi_ref, lo_ref in (
                (spline(fraction), w_hi, w_lo),
                (spline_rate(fraction), d_hi, d_lo),
            ):
                hi, lo = split(tap_table(first, values, 48))
                hi_ref[half, start : start + 48, lanes] = hi
                lo_ref[half, start : start + 48, lanes] = lo
        lanes = slice(half * WIN, (half + 1) * WIN)
        cells = split(product(spectrum, (y_hi[:, lanes], y_lo[:, lanes])))
        field[...] = product(cells, (w_hi[half], w_lo[half]))
        rate[...] = product(cells, (d_hi[half], d_lo[half]))
        for c in range(8):
            j = half * 8 + c
            lanes = slice(c * ATOMS, (c + 1) * ATOMS)
            row = lambda r: sites[j, r : r + 1, :]
            fraction_z = row(5)
            along, slant = z_modes(setup, row(2), [spline(fraction_z), spline_rate(fraction_z)])
            value = jnp.zeros((16, ATOMS), f32)
            over_z = jnp.zeros((16, ATOMS), f32)
            over_y = jnp.zeros((16, ATOMS), f32)
            for m in range(SLOTS):
                tile = field[m * 16 : (m + 1) * 16, lanes]
                value = value + along[m : m + 1, :] * tile
                over_z = over_z + slant[m : m + 1, :] * tile
                over_y = over_y + along[m : m + 1, :] * rate[m * 16 : (m + 1) * 16, lanes]
            table_x = tap_table(row(0) + 1.0, spline(row(3)), 16)
            rate_x = tap_table(row(0) + 1.0, spline_rate(row(3)), 16)
            gather = lambda x: jnp.sum(x, axis=0, keepdims=True)
            out[j] = jnp.concatenate(
                [
                    0.5 * gather(table_x * value),
                    -gather(rate_x * value),
                    -gather(table_x * over_y),
                    -gather(table_x * over_z),
                    jnp.zeros((4, ATOMS), f32),
                ],
                axis=0,
            )


def final_kernel(parts, own, energy, force):
    total = parts[0]
    for j in range(1, N_GY):
        total = total + parts[j]
    total = total * own[...]
    energy[...] = total[0:1, :]
    force[...] = total[1:4, :]


def shape(*dims):
    return jax.ShapeDtypeStruct(dims, f32)


def local(
    positions,
    neighbours,
    live_count,
    stencil_base,
    spline_weight,
    spline_slope,
    embed_scale,
    embed_bias,
    desc_gain,
    fit_in,
    fit_bias,
    fit_hidden,
    fit_bias_two,
    fit_out,
):
    ring = lambda axis, step: [
        (i, (i + step) % lax.axis_size(axis)) for i in range(lax.axis_size(axis))
    ]
    mine = positions.reshape(3, ATOMS)
    left = lax.ppermute(mine, "gy", ring("gy", 1))
    right = lax.ppermute(mine, "gy", ring("gy", -1))
    column = jnp.concatenate([left, mine, right], axis=0)
    before = lax.ppermute(column, "gx", ring("gx", 1))
    after = lax.ppermute(column, "gx", ring("gx", -1))

    widen = lambda v: jnp.pad(v, (0, 128 - v.shape[0]))
    none = jnp.zeros((128,), f32)
    packed = jnp.stack(
        [widen(embed_scale), widen(embed_bias), fit_bias, fit_bias_two, fit_out, none, none, none]
    )
    sites, own = pl.pallas_call(
        charge_kernel,
        name="charge",
        out_shape=(shape(N_GY, 8, ATOMS), shape(1, ATOMS)),
        in_specs=[SMEM] + vmem(10),
        out_specs=tuple(vmem(2)),
        scratch_shapes=[
            pltpu.VMEM((4, EMB_ROWS, ATOMS), f32),
            pltpu.VMEM((DESC, ATOMS), f32),
            pltpu.VMEM((DESC, ATOMS), bf16),
        ],
        compiler_params=PARAMS,
    )(
        live_count,
        before,
        column,
        after,
        neighbours.reshape(NEIGH, ATOMS),
        stencil_base.reshape(3, ATOMS),
        spline_weight.reshape(3, 4, ATOMS).transpose(1, 0, 2),
        packed,
        desc_gain.reshape(DESC, 1),
        fit_in,
        fit_hidden,
    )
    sites = lax.all_to_all(sites, "gy", 0, 0, tiled=True)

    device = lax.axis_index("gy").reshape(1)
    spread = pl.pallas_call(
        forward_kernel,
        name="forward",
        out_shape=shape(N_GX, 36, 128),
        in_specs=[SMEM] + vmem(3),
        out_specs=vmem(1)[0],
        scratch_shapes=[
            pltpu.VMEM((2, GRID, HALF), bf16),
            pltpu.VMEM((2, GRID, HALF), bf16),
            pltpu.VMEM((2, WIN, HALF), bf16),
            pltpu.VMEM((2, WIN, HALF), bf16),
            pltpu.VMEM((GRID, GRID), f32),
        ],
        compiler_params=PARAMS,
    )(device, sites, *Y_IN)
    spread = lax.all_to_all(spread, "gx", 0, 0, tiled=True)

    gx, gy = lax.axis_index("gx"), lax.axis_index("gy")
    slot = (gx // 4) * 3 + jnp.arange(3)
    freq_z = gy * 12 + slot % 12
    square_z = jnp.square(freq_z.astype(f32) * WAVE)
    weight_z = jnp.where(freq_z == 0, 1.0, 2.0) / GRID
    quarter = gx % 4
    square = square_z[:, None] + jnp.asarray(SQUARE_Y)[quarter]
    weight = weight_z[:, None] * jnp.asarray(WEIGHT_Y)[quarter]
    spread = pl.pallas_call(
        x_kernel,
        name="convolve",
        out_shape=shape(N_GX, 36, 128),
        in_specs=vmem(9),
        out_specs=vmem(1)[0],
        scratch_shapes=[pltpu.VMEM((N_GX * 16, GRID), f32)],
        compiler_params=PARAMS,
    )(square, weight, SQUARE_X, WEIGHT_X, *X_IN, *X_OUT, spread)
    spread = lax.all_to_all(spread, "gx", 0, 0, tiled=True)

    parts = pl.pallas_call(
        inverse_kernel,
        name="inverse",
        out_shape=shape(N_GY, 8, ATOMS),
        in_specs=[SMEM] + vmem(4),
        out_specs=vmem(1)[0],
        scratch_shapes=[
            pltpu.VMEM((GRID, GRID), f32),
            pltpu.VMEM((2, WIN, HALF), bf16),
            pltpu.VMEM((2, WIN, HALF), bf16),
            pltpu.VMEM((2, WIN, HALF), bf16),
            pltpu.VMEM((2, WIN, HALF), bf16),
            pltpu.VMEM((GRID, HALF), f32),
            pltpu.VMEM((GRID, HALF), f32),
        ],
        compiler_params=PARAMS,
    )(device, sites, *Y_OUT, spread)
    parts = lax.all_to_all(parts, "gy", 0, 0, tiled=True)
    energy, force = pl.pallas_call(
        final_kernel,
        name="finish",
        out_shape=(shape(1, ATOMS), shape(3, ATOMS)),
        in_specs=vmem(2),
        out_specs=tuple(vmem(2)),
        compiler_params=PARAMS,
    )(parts, own)
    return energy.reshape(1, 1, ATOMS), force.reshape(3, 1, 1, ATOMS)


def solution(mesh):
    placed = (
        P(None, "gx", "gy", None),
        P(None, "gx", "gy", None),
        P("gx", "gy"),
        P(None, "gx", "gy", None),
        P(None, None, "gx", "gy", None),
        P(None, None, "gx", "gy", None),
        P(),
        P(),
        P(),
        P(),
        P(),
        P(),
        P(),
        P(),
    )
    return jax.shard_map(
        local,
        mesh=mesh,
        in_specs=placed,
        out_specs=(P("gx", "gy", None), P(None, "gx", "gy", None)),
        check_vma=False,
    )
```

```python
import math

import jax
import jax.numpy as jnp
import numpy as np
from jax import lax
from jax.experimental import pallas as pl
from jax.experimental.pallas import tpu as pltpu
from jax.sharding import PartitionSpec as P

GRID = 384
AXIS = 16
ATOMS = 128
NEIGH = 32
EMB = 100
EMB_ROWS = 104
DESC = 1600
CX = 12
CY = 24
N_GX = 32
N_GY = 16
SLOTS = 24
LANES = 96
WIN = 64
PAIR = 256

radius_scale = 4.0
screen_width = 0.25
norm_floor = 1e-06
full_turn = 2.0 * math.pi
f32 = jnp.float32
bf16 = jnp.bfloat16


def axis_modes():
    cosines = [(k, 0) for k in range(193)]
    sines = [(k, 1) for k in range(1, 192)]
    modes = [m for odd in (0, 1) for m in cosines + sines if m[0] % 2 == odd]
    return np.array([k for k, _ in modes]), np.array([kind for _, kind in modes])


FREQ, IS_SINE = axis_modes()
WAVE = full_turn / GRID
SIDE = GRID // 2


def mode_table(cells):
    turn = (FREQ[:, None] * cells[None, :] - 96 * IS_SINE[:, None]) % GRID
    return np.cos(full_turn * turn / GRID)


def mode_weight(freq):
    return np.where((freq == 0) | (freq == GRID // 2), 1.0, 2.0) / GRID


def halves(table):
    table = table.astype(np.float32)
    upper = table.astype(jnp.bfloat16)
    lower = (table - upper.astype(np.float32)).astype(jnp.bfloat16)
    return upper, lower


def by_parity(table, stacked):
    out = []
    for part in (table[:SIDE], table[SIDE:]):
        pair = halves(part.T if stacked == "columns" else part)
        out.append(np.concatenate(pair, axis=0) if stacked != "none" else pair)
    return out


CELLS_X = (np.arange(16)[:, None] * CX + np.arange(16)[None, :] - 1).reshape(-1) % GRID
CELLS_Y = (np.arange(4)[:, None] * 2 * CY + np.arange(64)[None, :] - 1).reshape(-1) % GRID
TABLE_X = mode_table(CELLS_X)
TABLE_Y = mode_table(CELLS_Y)
X_IN = by_parity(TABLE_X, "rows")
X_OUT = by_parity(TABLE_X, "columns")
Y_IN = by_parity(TABLE_Y, "columns")
Y_OUT = by_parity(TABLE_Y, "rows")
SQUARE_X = np.broadcast_to(((FREQ * WAVE) ** 2)[:, None], (GRID, 128)).astype(np.float32)
WEIGHT_X = np.broadcast_to(mode_weight(FREQ)[:, None], (GRID, 128)).astype(np.float32)
SQUARE_Y = np.zeros((4, 1, 128), np.float32)
SQUARE_Y[:, 0, :LANES] = ((FREQ * WAVE) ** 2).reshape(4, LANES)
WEIGHT_Y = np.zeros((4, 1, 128), np.float32)
WEIGHT_Y[:, 0, :LANES] = mode_weight(FREQ).reshape(4, LANES)


def split(value):
    upper = value.astype(bf16)
    return upper, (value - upper.astype(f32)).astype(bf16)


def product(left, right, dims=(((1,), (0,)), ((), ()))):
    a, b = left
    c, d = right
    dot = lambda x, y: lax.dot_general(x, y, dims, preferred_element_type=f32)
    return dot(a, c) + (dot(a, d) + dot(b, c))


def vmem(count):
    return [pl.BlockSpec(memory_space=pltpu.VMEM)] * count


SMEM = pl.BlockSpec(memory_space=pltpu.SMEM)
PARAMS = pltpu.CompilerParams(vmem_limit_bytes=48 * 1024 * 1024)


def charge_kernel(
    count, before, middle, after, listed, base, weight, scale, bias, bias_one, bias_two, read_out,
    gain, fit_in, fit_hidden, sites, own, vectors, mixed, descriptor, normed,
):
    vectors[0:1, 0:EMB] = scale[...]
    vectors[1:2, 0:EMB] = bias[...]
    for k, ref in enumerate((bias_one, bias_two, read_out)):
        vectors[k + 2 : k + 3, :] = ref[...]
    entry = listed[...]
    block = lax.shift_right_logical(entry, 7)
    slot = jnp.bitwise_and(entry, ATOMS - 1)
    picked = [jnp.zeros((NEIGH, ATOMS), f32) for _ in range(3)]
    for a, rows in enumerate((before, middle, after)):
        for b in range(3):
            here = block == a * 3 + b
            for c, shift in enumerate(((a - 1) * CX, (b - 1) * CY, 0)):
                row = rows[b * 3 + c, 0] + float(shift)
                row = jnp.broadcast_to(row, (NEIGH, ATOMS))
                value = jnp.take_along_axis(row, slot, axis=1)
                picked[c] = jnp.where(here, value, picked[c])
    delta = [picked[c] - middle[3 + c, 0] for c in range(3)]
    radius = jnp.sqrt(delta[0] * delta[0] + delta[1] * delta[1] + delta[2] * delta[2])
    smooth = 1.0 / (1.0 + radius / radius_scale)
    factor = smooth / (radius + radius_scale)
    envelope = [smooth] + [d * factor for d in delta]

    columns = jnp.transpose(vectors[...])
    column = lambda k, lo, hi: jnp.broadcast_to(columns[lo:hi, k : k + 1], (hi - lo, ATOMS))
    for lo, hi in ((0, 32), (32, 64), (64, EMB_ROWS)):
        scale, bias = column(0, lo, hi), column(1, lo, hi)
        total = [jnp.zeros((hi - lo, ATOMS), f32) for _ in range(4)]
        for k in range(NEIGH):
            embed = jnp.tanh(smooth[k : k + 1, :] * scale + bias)
            for c in range(4):
                total[c] = total[c] + embed * envelope[c][k : k + 1, :]
        for c in range(4):
            mixed[c, lo:hi, :] = total[c]
    second_factor = [mixed[c, 0:AXIS, :] for c in range(4)]
    squares = jnp.zeros((AXIS, ATOMS), f32)
    for e in range(EMB):
        value = mixed[0, e : e + 1, :] * second_factor[0]
        for c in range(1, 4):
            value = value + mixed[c, e : e + 1, :] * second_factor[c]
        squares = squares + value * value
        descriptor[e * AXIS : (e + 1) * AXIS, :] = value
    mean = jnp.sum(squares, axis=0, keepdims=True) * (1.0 / DESC)
    scaling = lax.rsqrt(mean + norm_floor)
    for e in range(EMB):
        rows = slice(e * AXIS, (e + 1) * AXIS)
        value = descriptor[rows, :] * scaling * jnp.broadcast_to(gain[rows, :], (AXIS, ATOMS))
        normed[rows, :] = value.astype(bf16)
    first = jnp.tanh(
        lax.dot_general(
            fit_in[...], normed[...], (((0,), (0,)), ((), ())), preferred_element_type=f32
        )
        + column(2, 0, 128)
    )
    second = (
        jnp.tanh(
            jnp.dot(fit_hidden[...], first.astype(bf16), preferred_element_type=f32)
            + column(3, 0, 128)
        )
        + first
    )
    charge = jnp.sum(column(4, 0, 128) * second, axis=0, keepdims=True)
    place = lax.broadcasted_iota(jnp.int32, (1, ATOMS), 1)
    charge = jnp.where(place < count[0, 0], charge, 0.0)
    own[0] = charge
    cell = [base[c, 0].astype(f32) for c in range(3)]
    fraction = [
        weight[c, 1, 0] + 2.0 * weight[c, 2, 0] + 3.0 * weight[c, 3, 0] - 1.0 for c in range(3)
    ]
    record = jnp.concatenate(cell + fraction + [charge, jnp.zeros((1, ATOMS), f32)], axis=0)
    for j in range(N_GY):
        sites[j] = record


def spline(fraction):
    remain = 1.0 - fraction
    square = fraction * fraction
    cube = square * fraction
    return [
        remain * remain * remain * (1.0 / 6.0),
        (3.0 * cube - 6.0 * square + 4.0) * (1.0 / 6.0),
        (-3.0 * cube + 3.0 * square + 3.0 * fraction + 1.0) * (1.0 / 6.0),
        cube * (1.0 / 6.0),
    ]


def spline_rate(fraction):
    remain = 1.0 - fraction
    square = fraction * fraction
    return [
        -0.5 * remain * remain,
        (3.0 * square - 4.0 * fraction) * 0.5,
        (-3.0 * square + 2.0 * fraction + 1.0) * 0.5,
        0.5 * square,
    ]


def tap_table(first, values, rows):
    away = lax.broadcasted_iota(jnp.int32, (rows, ATOMS), 0).astype(f32) - first
    total = jnp.zeros((rows, ATOMS), f32)
    for t, value in enumerate(values):
        total = jnp.where(away == float(t), value, total)
    return total


def cos_sin(step):
    step = step - GRID * jnp.round(step * (1.0 / GRID))
    quarter = jnp.round(step * (1.0 / 96.0))
    angle = (step - 96.0 * quarter) * WAVE
    square = angle * angle
    sine = angle * (
        1.0 + square * (-1.0 / 6 + square * (1.0 / 120 + square * (-1.0 / 5040 + square / 362880)))
    )
    cosine = 1.0 + square * (
        -0.5 + square * (1.0 / 24 + square * (-1.0 / 720 + square * (1.0 / 40320 - square / 3628800)))
    )
    odd = jnp.abs(quarter) == 1.0
    straight = jnp.where(jnp.abs(quarter) == 2.0, -1.0, 1.0)
    turned = jnp.where(odd, quarter, straight)
    cos_value = jnp.where(odd, -sine, cosine) * turned
    sin_value = jnp.where(odd, cosine, sine) * turned
    return cos_value, sin_value


def z_setup(device):
    row = lax.broadcasted_iota(jnp.int32, (SLOTS, ATOMS), 0)
    is_sine = row >= 12
    freq = (device * 12 + jnp.where(is_sine, row - 12, row)).astype(f32)
    phase = jnp.where(is_sine, 96.0, 0.0)
    turns = [cos_sin(freq * float(t)) for t in range(4)]
    return freq, phase, turns


def z_modes(setup, base, lists):
    freq, phase, turns = setup
    cosine, sine = cos_sin(freq * base - phase)
    out = []
    for values in lists:
        along = values[0] + sum(values[t] * turns[t][0] for t in range(1, 4))
        across = sum(values[t] * turns[t][1] for t in range(1, 4))
        out.append(cosine * along - sine * across)
    return out


def pair_table(sites, j, values):
    first = sites[j, 1:2, :] + (1.0 + CY * (j % 2))
    lo, hi = (0, 32) if j % 2 == 0 else (16, 64)
    table = tap_table(first - float(lo), values, hi - lo)
    pieces = [jnp.zeros((lo, ATOMS), f32)] if lo else []
    pieces.append(table)
    if hi < WIN:
        pieces.append(jnp.zeros((WIN - hi, ATOMS), f32))
    return split(jnp.concatenate(pieces, axis=0))


def first_half():
    return lax.broadcasted_iota(jnp.int32, (GRID, 128), 1) < WIN


def forward_kernel(device, sites, even, odd, out, u_hi, u_lo, w, held):
    setup = z_setup(device[0])
    cells = []
    for pair in range(8):
        for c in range(2):
            j = pair * 2 + c
            lanes = slice(c * ATOMS, (c + 1) * ATOMS)
            row = lambda r: sites[j, r : r + 1, :]
            weight_x = [v * row(6) for v in spline(row(3))]
            table_x = tap_table(row(0) + 1.0, weight_x, 16)
            hi, lo = pair_table(sites, j, spline(row(4)))
            w[pair, 0:WIN, lanes] = hi
            w[pair, WIN:, lanes] = lo
            (along_z,) = z_modes(setup, row(2), [spline(row(5))])
            for m in range(SLOTS):
                hi, lo = split(along_z[m : m + 1, :] * table_x)
                u_hi[pair, m * 16 : (m + 1) * 16, lanes] = hi
                u_lo[pair, m * 16 : (m + 1) * 16, lanes] = lo
        dims = (((1,), (1,)), ((), ()))
        both = lax.dot_general(u_hi[pair], w[pair], dims, preferred_element_type=f32)
        both = both + lax.dot_general(u_lo[pair], w[pair], dims, preferred_element_type=f32)
        cells.append(both + pltpu.roll(both, WIN, 1))
    front = first_half()
    tiles = [jnp.where(front, cells[2 * t], cells[2 * t + 1]) for t in range(4)]
    for parity, table in enumerate((even, odd)):
        sign = 1.0 - 2.0 * parity
        near = jnp.concatenate([tiles[0] + sign * tiles[2], tiles[1] + sign * tiles[3]], axis=1)
        held[...] = product(split(near), (table[0:256, :], table[256:512, :]))
        for side in range(2):
            kq = parity * 2 + side
            block = held[:, side * LANES : (side + 1) * LANES]
            for sg in range(8):
                out[sg * 4 + kq, :, 0:LANES] = block[sg * 48 : sg * 48 + 36, :]
                for p in range(3):
                    out[sg * 4 + kq, 12 * p : 12 * p + 12, LANES:128] = block[
                        sg * 48 + 36 : sg * 48 + 48, 32 * p : 32 * p + 32
                    ]


def x_kernel(square, weight, sx, wx, in_even, in_odd, out_even, out_odd, got, out, held):
    for i in range(N_GX):
        rows = slice(i * 16, (i + 1) * 16)
        for q in range(2):
            held[rows, q * 128 : q * 128 + LANES] = got[i, 16 * q : 16 * q + 16, 0:LANES]
        lane = 2 * 128
        held[i * 16 : i * 16 + 4, lane : lane + LANES] = got[i, 32:36, 0:LANES]
        for p in range(3):
            held[i * 16 + 4 : i * 16 + 16, lane + 32 * p : lane + 32 * p + 32] = got[
                i, 12 * p : 12 * p + 12, LANES:128
            ]
    dot = lambda x, y: jnp.dot(x, y, preferred_element_type=f32)
    near, far = held[0:256, :], held[256:512, :]
    result = []
    for parity, (table_in, table_out) in enumerate(((in_even, out_even), (in_odd, out_odd))):
        hi, lo = split(near + far if parity == 0 else near - far)
        both = dot(table_in[...], hi)
        modes = both[0:SIDE, :] + (both[SIDE:, :] + dot(table_in[0:SIDE, :], lo))
        rows = slice(parity * SIDE, (parity + 1) * SIDE)
        scaled = []
        for q in range(3):
            wave = sx[rows, :] + square[q : q + 1, :]
            safe = jnp.where(wave > 0, wave, 1.0)
            green = 2.0 * full_turn * jnp.exp(-0.5 * screen_width * screen_width * wave) / safe
            green = jnp.where(wave > 0, green, 0.0) * (wx[rows, :] * weight[q : q + 1, :])
            scaled.append(modes[:, q * 128 : (q + 1) * 128] * green)
        hi, lo = split(jnp.concatenate(scaled, axis=1))
        both = dot(table_out[...], hi)
        result.append(both[0:256, :] + (both[256:, :] + dot(table_out[0:256, :], lo)))
    held[0:256, :] = result[0] + result[1]
    held[256:512, :] = result[0] - result[1]
    for i in range(N_GX):
        rows = slice(i * 16, (i + 1) * 16)
        for q in range(2):
            out[i, 16 * q : 16 * q + 16, 0:LANES] = held[rows, q * 128 : q * 128 + LANES]
        lane = 2 * 128
        out[i, 32:36, 0:LANES] = held[i * 16 : i * 16 + 4, lane : lane + LANES]
        for p in range(3):
            out[i, 12 * p : 12 * p + 12, LANES:128] = held[
                i * 16 + 4 : i * 16 + 16, lane + 32 * p : lane + 32 * p + 32
            ]


def inverse_kernel(device, sites, even, odd, got, out, modes, w, d, field, rate):
    setup = z_setup(device[0])
    for kq in range(4):
        part, side = kq // 2, (kq % 2) * LANES
        for sg in range(8):
            row = sg * 48
            modes[part, row : row + 36, side : side + LANES] = got[sg * 4 + kq, :, 0:LANES]
            for p in range(3):
                modes[part, row + 36 : row + 48, side + 32 * p : side + 32 * p + 32] = got[
                    sg * 4 + kq, 12 * p : 12 * p + 12, LANES:128
                ]
    parts = [
        product(split(modes[p]), (table[0:SIDE, :], table[SIDE:, :]))
        for p, table in enumerate((even, odd))
    ]
    halves_y = [parts[0] + parts[1], parts[0] - parts[1]]
    front = first_half()
    for half in range(2):
        for tile in range(2):
            cells = halves_y[half][:, tile * 128 : (tile + 1) * 128]
            turned = pltpu.roll(cells, WIN, 1)
            for p, (near, far) in enumerate(((cells, turned), (turned, cells))):
                pair = half * 4 + tile * 2 + p
                upper = near.astype(bf16).astype(f32)
                lower = far - far.astype(bf16).astype(f32)
                mixed = jnp.where(front, upper, lower).astype(bf16)
                mixed = jnp.concatenate([mixed, mixed], axis=1)
                for c in range(2):
                    j = pair * 2 + c
                    lanes = slice(c * ATOMS, (c + 1) * ATOMS)
                    fraction = sites[j, 4:5, :]
                    for values, ref in ((spline(fraction), w), (spline_rate(fraction), d)):
                        hi, lo = pair_table(sites, j, values)
                        ref[pair, 0:WIN, lanes] = hi
                        ref[pair, WIN : 2 * WIN, lanes] = hi
                        ref[pair, 2 * WIN : 3 * WIN, lanes] = lo
                        ref[pair, 3 * WIN :, lanes] = lo
                field[pair % 2] = jnp.dot(mixed, w[pair], preferred_element_type=f32)
                rate[pair % 2] = jnp.dot(mixed, d[pair], preferred_element_type=f32)
                for c in range(2):
                    j = pair * 2 + c
                    lanes = slice(c * ATOMS, (c + 1) * ATOMS)
                    row = lambda r: sites[j, r : r + 1, :]
                    taps_z = [spline(row(5)), spline_rate(row(5))]
                    along, slant = z_modes(setup, row(2), taps_z)
                    value = jnp.zeros((16, ATOMS), f32)
                    over_z = jnp.zeros((16, ATOMS), f32)
                    over_y = jnp.zeros((16, ATOMS), f32)
                    for m in range(SLOTS):
                        rows = slice(m * 16, (m + 1) * 16)
                        here = field[pair % 2, rows, lanes]
                        value = value + along[m : m + 1, :] * here
                        over_z = over_z + slant[m : m + 1, :] * here
                        over_y = over_y + along[m : m + 1, :] * rate[pair % 2, rows, lanes]
                    table_x = tap_table(row(0) + 1.0, spline(row(3)), 16)
                    rate_x = tap_table(row(0) + 1.0, spline_rate(row(3)), 16)
                    gather = lambda x: jnp.sum(x, axis=0, keepdims=True)
                    out[j] = jnp.concatenate(
                        [
                            0.5 * gather(table_x * value),
                            -gather(rate_x * value),
                            -gather(table_x * over_y),
                            -gather(table_x * over_z),
                            jnp.zeros((4, ATOMS), f32),
                        ],
                        axis=0,
                    )


def final_kernel(parts, own, energy, force):
    total = parts[0]
    for j in range(1, N_GY):
        total = total + parts[j]
    total = total * own[0]
    energy[0] = total[0:1, :]
    for c in range(3):
        force[c, 0] = total[c + 1 : c + 2, :]


def shape(*dims):
    return jax.ShapeDtypeStruct(dims, f32)


def local(
    positions,
    neighbours,
    live_count,
    stencil_base,
    spline_weight,
    spline_slope,
    embed_scale,
    embed_bias,
    desc_gain,
    fit_in,
    fit_bias,
    fit_hidden,
    fit_bias_two,
    fit_out,
):
    ring = lambda axis, step: [
        (i, (i + step) % lax.axis_size(axis)) for i in range(lax.axis_size(axis))
    ]
    left = lax.ppermute(positions, "gy", ring("gy", 1))
    right = lax.ppermute(positions, "gy", ring("gy", -1))
    column = jnp.concatenate([left, positions, right], axis=0)
    before = lax.ppermute(column, "gx", ring("gx", 1))
    after = lax.ppermute(column, "gx", ring("gx", -1))

    gx, gy = lax.axis_index("gx"), lax.axis_index("gy")
    device = gy.reshape(1)
    slot = (gx // 4) * 3 + jnp.arange(3)
    freq_z = gy * 12 + slot % 12
    square_z = jnp.square(freq_z.astype(f32) * WAVE)
    weight_z = jnp.where(freq_z == 0, 1.0, 2.0) / GRID
    quarter = gx % 4
    square = square_z[:, None] + jnp.asarray(SQUARE_Y)[quarter]
    weight = weight_z[:, None] * jnp.asarray(WEIGHT_Y)[quarter]
    middle, gain, device, square, weight = lax.optimization_barrier(
        (column, desc_gain.reshape(DESC, 1), device, square, weight)
    )
    sites, own = pl.pallas_call(
        charge_kernel,
        name="charge",
        out_shape=(shape(N_GY, 8, ATOMS), shape(1, 1, ATOMS)),
        in_specs=[SMEM] + vmem(14),
        out_specs=tuple(vmem(2)),
        scratch_shapes=[
            pltpu.VMEM((8, ATOMS), f32),
            pltpu.VMEM((4, EMB_ROWS, ATOMS), f32),
            pltpu.VMEM((DESC, ATOMS), f32),
            pltpu.VMEM((DESC, ATOMS), bf16),
        ],
        compiler_params=PARAMS,
    )(
        live_count,
        before,
        middle,
        after,
        neighbours.reshape(NEIGH, ATOMS),
        stencil_base.reshape(3, 1, 1, ATOMS),
        spline_weight,
        embed_scale.reshape(1, EMB),
        embed_bias.reshape(1, EMB),
        fit_bias.reshape(1, 128),
        fit_bias_two.reshape(1, 128),
        fit_out.reshape(1, 128),
        gain,
        fit_in.T,
        fit_hidden,
    )
    sites = lax.all_to_all(sites, "gy", 0, 0, tiled=True)

    spread = pl.pallas_call(
        forward_kernel,
        name="forward",
        out_shape=shape(N_GX, 36, 128),
        in_specs=[SMEM] + vmem(3),
        out_specs=vmem(1)[0],
        scratch_shapes=[
            pltpu.VMEM((8, GRID, PAIR), bf16),
            pltpu.VMEM((8, GRID, PAIR), bf16),
            pltpu.VMEM((8, 2 * WIN, PAIR), bf16),
            pltpu.VMEM((GRID, SIDE), f32),
        ],
        compiler_params=PARAMS,
    )(device, sites, *Y_IN)
    spread = lax.all_to_all(spread, "gx", 0, 0, tiled=True)

    spread = pl.pallas_call(
        x_kernel,
        name="convolve",
        out_shape=shape(N_GX, 36, 128),
        in_specs=vmem(9),
        out_specs=vmem(1)[0],
        scratch_shapes=[pltpu.VMEM((N_GX * 16, GRID), f32)],
        compiler_params=PARAMS,
    )(square, weight, SQUARE_X, WEIGHT_X, *X_IN, *X_OUT, spread)
    spread = lax.all_to_all(spread, "gx", 0, 0, tiled=True)

    parts = pl.pallas_call(
        inverse_kernel,
        name="inverse",
        out_shape=shape(N_GY, 8, ATOMS),
        in_specs=[SMEM] + vmem(4),
        out_specs=vmem(1)[0],
        scratch_shapes=[
            pltpu.VMEM((2, GRID, SIDE), f32),
            pltpu.VMEM((8, 4 * WIN, PAIR), bf16),
            pltpu.VMEM((8, 4 * WIN, PAIR), bf16),
            pltpu.VMEM((2, GRID, PAIR), f32),
            pltpu.VMEM((2, GRID, PAIR), f32),
        ],
        compiler_params=PARAMS,
    )(device, sites, *Y_OUT, spread)
    parts = lax.all_to_all(parts, "gy", 0, 0, tiled=True)
    energy, force = pl.pallas_call(
        final_kernel,
        name="finish",
        out_shape=(shape(1, 1, ATOMS), shape(3, 1, 1, ATOMS)),
        in_specs=vmem(2),
        out_specs=tuple(vmem(2)),
        compiler_params=PARAMS,
    )(parts, own)
    return energy, force


def solution(mesh):
    placed = (
        P(None, "gx", "gy", None),
        P(None, "gx", "gy", None),
        P("gx", "gy"),
        P(None, "gx", "gy", None),
        P(None, None, "gx", "gy", None),
        P(None, None, "gx", "gy", None),
        P(),
        P(),
        P(),
        P(),
        P(),
        P(),
        P(),
        P(),
    )
    return jax.shard_map(
        local,
        mesh=mesh,
        in_specs=placed,
        out_specs=(P("gx", "gy", None), P(None, "gx", "gy", None)),
        check_vma=False,
    )
```

```python
import math

import jax
import jax.numpy as jnp
import numpy as np
from jax import lax
from jax.experimental import pallas as pl
from jax.experimental.pallas import tpu as pltpu
from jax.sharding import PartitionSpec as P

GRID = 384
AXIS = 16
ATOMS = 128
NEIGH = 32
EMB = 100
EMB_ROWS = 104
DESC = 1600
CX = 12
CY = 24
N_GX = 32
N_GY = 16
SLOTS = 24
LANES = 96
WIN = 64
PAIR = 256

radius_scale = 4.0
screen_width = 0.25
norm_floor = 1e-06
full_turn = 2.0 * math.pi
f32 = jnp.float32
bf16 = jnp.bfloat16


def axis_modes():
    cosines = [(k, 0) for k in range(193)]
    sines = [(k, 1) for k in range(1, 192)]
    modes = [m for odd in (0, 1) for m in cosines + sines if m[0] % 2 == odd]
    return np.array([k for k, _ in modes]), np.array([kind for _, kind in modes])


FREQ, IS_SINE = axis_modes()
WAVE = full_turn / GRID
SIDE = GRID // 2


def mode_table(cells):
    turn = (FREQ[:, None] * cells[None, :] - 96 * IS_SINE[:, None]) % GRID
    return np.cos(full_turn * turn / GRID)


def mode_weight(freq):
    return np.where((freq == 0) | (freq == GRID // 2), 1.0, 2.0) / GRID


def halves(table):
    table = table.astype(np.float32)
    upper = table.astype(jnp.bfloat16)
    lower = (table - upper.astype(np.float32)).astype(jnp.bfloat16)
    return upper, lower


def by_parity(table, stacked):
    out = []
    for part in (table[:SIDE], table[SIDE:]):
        pair = halves(part.T if stacked == "columns" else part)
        out.append(np.concatenate(pair, axis=0) if stacked != "none" else pair)
    return out


CELLS_X = (np.arange(16)[:, None] * CX + np.arange(16)[None, :] - 1).reshape(-1) % GRID
CELLS_Y = (np.arange(4)[:, None] * 2 * CY + np.arange(64)[None, :] - 1).reshape(-1) % GRID
TABLE_X = mode_table(CELLS_X)
TABLE_Y = mode_table(CELLS_Y)
X_IN = by_parity(TABLE_X, "rows")
X_OUT = by_parity(TABLE_X, "columns")
Y_IN = by_parity(TABLE_Y, "columns")
Y_OUT = by_parity(TABLE_Y, "rows")
SQUARE_X = np.broadcast_to(((FREQ * WAVE) ** 2)[:, None], (GRID, 128)).astype(np.float32)
WEIGHT_X = np.broadcast_to(mode_weight(FREQ)[:, None], (GRID, 128)).astype(np.float32)
SQUARE_Y = np.zeros((4, 1, 128), np.float32)
SQUARE_Y[:, 0, :LANES] = ((FREQ * WAVE) ** 2).reshape(4, LANES)
WEIGHT_Y = np.zeros((4, 1, 128), np.float32)
WEIGHT_Y[:, 0, :LANES] = mode_weight(FREQ).reshape(4, LANES)


def split(value):
    upper = value.astype(bf16)
    return upper, (value - upper.astype(f32)).astype(bf16)


def product(left, right, dims=(((1,), (0,)), ((), ()))):
    a, b = left
    c, d = right
    dot = lambda x, y: lax.dot_general(x, y, dims, preferred_element_type=f32)
    return dot(a, c) + (dot(a, d) + dot(b, c))


def vmem(count):
    return [pl.BlockSpec(memory_space=pltpu.VMEM)] * count


SMEM = pl.BlockSpec(memory_space=pltpu.SMEM)
PARAMS = pltpu.CompilerParams(vmem_limit_bytes=48 * 1024 * 1024)


def charge_kernel(
    count, parity, chip, middle, core, listed, base, weight, scale, bias, bias_one, bias_two, read_out,
    gain, fit_in, fit_hidden, sites, own, vectors, mixed, descriptor, normed,
):
    vectors[0:1, 0:EMB] = scale[...]
    vectors[1:2, 0:EMB] = bias[...]
    for k, ref in enumerate((bias_one, bias_two, read_out)):
        vectors[k + 2 : k + 3, :] = ref[...]
    entry = listed[...]
    block = lax.shift_right_logical(entry, 7)
    slot = jnp.bitwise_and(entry, ATOMS - 1)
    picked = [jnp.zeros((NEIGH, ATOMS), f32) for _ in range(3)]
    is_even = jnp.full((1, ATOMS), parity[0], jnp.int32) == 0
    rows_of = (
        lambda r: jnp.where(is_even, chip[r, 0], core[r, 0]),
        lambda r: middle[r, 0],
        lambda r: jnp.where(is_even, core[r, 0], chip[r, 0]),
    )
    for a, rows in enumerate(rows_of):
        for b in range(3):
            here = block == a * 3 + b
            for c, shift in enumerate(((a - 1) * CX, (b - 1) * CY, 0)):
                row = rows(b * 3 + c) + float(shift)
                row = jnp.broadcast_to(row, (NEIGH, ATOMS))
                value = jnp.take_along_axis(row, slot, axis=1)
                picked[c] = jnp.where(here, value, picked[c])
    delta = [picked[c] - middle[3 + c, 0] for c in range(3)]
    radius = jnp.sqrt(delta[0] * delta[0] + delta[1] * delta[1] + delta[2] * delta[2])
    smooth = 1.0 / (1.0 + radius / radius_scale)
    factor = smooth / (radius + radius_scale)
    envelope = [smooth] + [d * factor for d in delta]

    columns = jnp.transpose(vectors[...])
    column = lambda k, lo, hi: jnp.broadcast_to(columns[lo:hi, k : k + 1], (hi - lo, ATOMS))
    for lo, hi in ((0, 32), (32, 64), (64, EMB_ROWS)):
        scale, bias = column(0, lo, hi), column(1, lo, hi)
        total = [jnp.zeros((hi - lo, ATOMS), f32) for _ in range(4)]
        for k in range(NEIGH):
            embed = jnp.tanh(smooth[k : k + 1, :] * scale + bias)
            for c in range(4):
                total[c] = total[c] + embed * envelope[c][k : k + 1, :]
        for c in range(4):
            mixed[c, lo:hi, :] = total[c]
    second_factor = [mixed[c, 0:AXIS, :] for c in range(4)]
    squares = jnp.zeros((AXIS, ATOMS), f32)
    for e in range(EMB):
        value = mixed[0, e : e + 1, :] * second_factor[0]
        for c in range(1, 4):
            value = value + mixed[c, e : e + 1, :] * second_factor[c]
        squares = squares + value * value
        descriptor[e * AXIS : (e + 1) * AXIS, :] = value
    mean = jnp.sum(squares, axis=0, keepdims=True) * (1.0 / DESC)
    scaling = lax.rsqrt(mean + norm_floor)
    for e in range(EMB):
        rows = slice(e * AXIS, (e + 1) * AXIS)
        value = descriptor[rows, :] * scaling * jnp.broadcast_to(gain[rows, :], (AXIS, ATOMS))
        normed[rows, :] = value.astype(bf16)
    first = jnp.tanh(
        lax.dot_general(
            fit_in[...], normed[...], (((0,), (0,)), ((), ())), preferred_element_type=f32
        )
        + column(2, 0, 128)
    )
    second = (
        jnp.tanh(
            jnp.dot(fit_hidden[...], first.astype(bf16), preferred_element_type=f32)
            + column(3, 0, 128)
        )
        + first
    )
    charge = jnp.sum(column(4, 0, 128) * second, axis=0, keepdims=True)
    place = lax.broadcasted_iota(jnp.int32, (1, ATOMS), 1)
    charge = jnp.where(place < count[0, 0], charge, 0.0)
    own[0] = charge
    cell = [base[c, 0].astype(f32) for c in range(3)]
    fraction = [
        weight[c, 1, 0] + 2.0 * weight[c, 2, 0] + 3.0 * weight[c, 3, 0] - 1.0 for c in range(3)
    ]
    record = jnp.concatenate(cell + fraction + [charge, jnp.zeros((1, ATOMS), f32)], axis=0)
    for j in range(N_GY):
        sites[j] = record


def spline(fraction):
    remain = 1.0 - fraction
    square = fraction * fraction
    cube = square * fraction
    return [
        remain * remain * remain * (1.0 / 6.0),
        (3.0 * cube - 6.0 * square + 4.0) * (1.0 / 6.0),
        (-3.0 * cube + 3.0 * square + 3.0 * fraction + 1.0) * (1.0 / 6.0),
        cube * (1.0 / 6.0),
    ]


def spline_rate(fraction):
    remain = 1.0 - fraction
    square = fraction * fraction
    return [
        -0.5 * remain * remain,
        (3.0 * square - 4.0 * fraction) * 0.5,
        (-3.0 * square + 2.0 * fraction + 1.0) * 0.5,
        0.5 * square,
    ]


def tap_table(first, values, rows):
    away = lax.broadcasted_iota(jnp.int32, (rows, ATOMS), 0).astype(f32) - first
    total = jnp.zeros((rows, ATOMS), f32)
    for t, value in enumerate(values):
        total = jnp.where(away == float(t), value, total)
    return total


def cos_sin(step):
    step = step - GRID * jnp.round(step * (1.0 / GRID))
    quarter = jnp.round(step * (1.0 / 96.0))
    angle = (step - 96.0 * quarter) * WAVE
    square = angle * angle
    sine = angle * (
        1.0 + square * (-1.0 / 6 + square * (1.0 / 120 + square * (-1.0 / 5040 + square / 362880)))
    )
    cosine = 1.0 + square * (
        -0.5 + square * (1.0 / 24 + square * (-1.0 / 720 + square * (1.0 / 40320 - square / 3628800)))
    )
    odd = jnp.abs(quarter) == 1.0
    straight = jnp.where(jnp.abs(quarter) == 2.0, -1.0, 1.0)
    turned = jnp.where(odd, quarter, straight)
    cos_value = jnp.where(odd, -sine, cosine) * turned
    sin_value = jnp.where(odd, cosine, sine) * turned
    return cos_value, sin_value


def z_setup(device):
    row = lax.broadcasted_iota(jnp.int32, (SLOTS, ATOMS), 0)
    is_sine = row >= 12
    freq = (device * 12 + jnp.where(is_sine, row - 12, row)).astype(f32)
    phase = jnp.where(is_sine, 96.0, 0.0)
    turns = [cos_sin(freq * float(t)) for t in range(4)]
    return freq, phase, turns


def z_modes(setup, base, lists):
    freq, phase, turns = setup
    cosine, sine = cos_sin(freq * base - phase)
    out = []
    for values in lists:
        along = values[0] + sum(values[t] * turns[t][0] for t in range(1, 4))
        across = sum(values[t] * turns[t][1] for t in range(1, 4))
        out.append(cosine * along - sine * across)
    return out


def pair_table(sites, j, values):
    first = sites[j, 1:2, :] + (1.0 + CY * (j % 2))
    lo, hi = (0, 32) if j % 2 == 0 else (16, 64)
    table = tap_table(first - float(lo), values, hi - lo)
    pieces = [jnp.zeros((lo, ATOMS), f32)] if lo else []
    pieces.append(table)
    if hi < WIN:
        pieces.append(jnp.zeros((WIN - hi, ATOMS), f32))
    return split(jnp.concatenate(pieces, axis=0))


def first_half():
    return lax.broadcasted_iota(jnp.int32, (GRID, 128), 1) < WIN


def forward_kernel(device, sites, even, odd, out, u_hi, u_lo, w, held):
    setup = z_setup(device[0])
    cells = []
    for pair in range(8):
        for c in range(2):
            j = pair * 2 + c
            lanes = slice(c * ATOMS, (c + 1) * ATOMS)
            row = lambda r: sites[j, r : r + 1, :]
            weight_x = [v * row(6) for v in spline(row(3))]
            table_x = tap_table(row(0) + 1.0, weight_x, 16)
            hi, lo = pair_table(sites, j, spline(row(4)))
            w[pair, 0:WIN, lanes] = hi
            w[pair, WIN:, lanes] = lo
            (along_z,) = z_modes(setup, row(2), [spline(row(5))])
            for m in range(SLOTS):
                hi, lo = split(along_z[m : m + 1, :] * table_x)
                u_hi[pair, m * 16 : (m + 1) * 16, lanes] = hi
                u_lo[pair, m * 16 : (m + 1) * 16, lanes] = lo
        dims = (((1,), (1,)), ((), ()))
        both = lax.dot_general(u_hi[pair], w[pair], dims, preferred_element_type=f32)
        both = both + lax.dot_general(u_lo[pair], w[pair], dims, preferred_element_type=f32)
        cells.append(both + pltpu.roll(both, WIN, 1))
    front = first_half()
    tiles = [jnp.where(front, cells[2 * t], cells[2 * t + 1]) for t in range(4)]
    for parity, table in enumerate((even, odd)):
        sign = 1.0 - 2.0 * parity
        near = jnp.concatenate([tiles[0] + sign * tiles[2], tiles[1] + sign * tiles[3]], axis=1)
        held[...] = product(split(near), (table[0:256, :], table[256:512, :]))
        for side in range(2):
            kq = parity * 2 + side
            block = held[:, side * LANES : (side + 1) * LANES]
            for sg in range(8):
                out[sg * 4 + kq, :, 0:LANES] = block[sg * 48 : sg * 48 + 36, :]
                for p in range(3):
                    out[sg * 4 + kq, 12 * p : 12 * p + 12, LANES:128] = block[
                        sg * 48 + 36 : sg * 48 + 48, 32 * p : 32 * p + 32
                    ]


def x_kernel(square, weight, sx, wx, in_even, in_odd, out_even, out_odd, got, out, held):
    for i in range(N_GX):
        rows = slice(i * 16, (i + 1) * 16)
        for q in range(2):
            held[rows, q * 128 : q * 128 + LANES] = got[i, 16 * q : 16 * q + 16, 0:LANES]
        lane = 2 * 128
        held[i * 16 : i * 16 + 4, lane : lane + LANES] = got[i, 32:36, 0:LANES]
        for p in range(3):
            held[i * 16 + 4 : i * 16 + 16, lane + 32 * p : lane + 32 * p + 32] = got[
                i, 12 * p : 12 * p + 12, LANES:128
            ]
    dot = lambda x, y: jnp.dot(x, y, preferred_element_type=f32)
    near, far = held[0:256, :], held[256:512, :]
    result = []
    for parity, (table_in, table_out) in enumerate(((in_even, out_even), (in_odd, out_odd))):
        hi, lo = split(near + far if parity == 0 else near - far)
        both = dot(table_in[...], hi)
        modes = both[0:SIDE, :] + (both[SIDE:, :] + dot(table_in[0:SIDE, :], lo))
        rows = slice(parity * SIDE, (parity + 1) * SIDE)
        scaled = []
        for q in range(3):
            wave = sx[rows, :] + square[q : q + 1, :]
            safe = jnp.where(wave > 0, wave, 1.0)
            green = 2.0 * full_turn * jnp.exp(-0.5 * screen_width * screen_width * wave) / safe
            green = jnp.where(wave > 0, green, 0.0) * (wx[rows, :] * weight[q : q + 1, :])
            scaled.append(modes[:, q * 128 : (q + 1) * 128] * green)
        hi, lo = split(jnp.concatenate(scaled, axis=1))
        both = dot(table_out[...], hi)
        result.append(both[0:256, :] + (both[256:, :] + dot(table_out[0:256, :], lo)))
    held[0:256, :] = result[0] + result[1]
    held[256:512, :] = result[0] - result[1]
    for i in range(N_GX):
        rows = slice(i * 16, (i + 1) * 16)
        for q in range(2):
            out[i, 16 * q : 16 * q + 16, 0:LANES] = held[rows, q * 128 : q * 128 + LANES]
        lane = 2 * 128
        out[i, 32:36, 0:LANES] = held[i * 16 : i * 16 + 4, lane : lane + LANES]
        for p in range(3):
            out[i, 12 * p : 12 * p + 12, LANES:128] = held[
                i * 16 + 4 : i * 16 + 16, lane + 32 * p : lane + 32 * p + 32
            ]


def inverse_kernel(device, sites, even, odd, got, out, modes, w, d, field, rate):
    setup = z_setup(device[0])
    for kq in range(4):
        part, side = kq // 2, (kq % 2) * LANES
        for sg in range(8):
            row = sg * 48
            modes[part, row : row + 36, side : side + LANES] = got[sg * 4 + kq, :, 0:LANES]
            for p in range(3):
                modes[part, row + 36 : row + 48, side + 32 * p : side + 32 * p + 32] = got[
                    sg * 4 + kq, 12 * p : 12 * p + 12, LANES:128
                ]
    parts = [
        product(split(modes[p]), (table[0:SIDE, :], table[SIDE:, :]))
        for p, table in enumerate((even, odd))
    ]
    halves_y = [parts[0] + parts[1], parts[0] - parts[1]]
    front = first_half()
    for half in range(2):
        for tile in range(2):
            cells = halves_y[half][:, tile * 128 : (tile + 1) * 128]
            turned = pltpu.roll(cells, WIN, 1)
            for p, (near, far) in enumerate(((cells, turned), (turned, cells))):
                pair = half * 4 + tile * 2 + p
                upper = near.astype(bf16).astype(f32)
                lower = far - far.astype(bf16).astype(f32)
                mixed = jnp.where(front, upper, lower).astype(bf16)
                mixed = jnp.concatenate([mixed, mixed], axis=1)
                for c in range(2):
                    j = pair * 2 + c
                    lanes = slice(c * ATOMS, (c + 1) * ATOMS)
                    fraction = sites[j, 4:5, :]
                    for values, ref in ((spline(fraction), w), (spline_rate(fraction), d)):
                        hi, lo = pair_table(sites, j, values)
                        ref[pair, 0:WIN, lanes] = hi
                        ref[pair, WIN : 2 * WIN, lanes] = hi
                        ref[pair, 2 * WIN : 3 * WIN, lanes] = lo
                        ref[pair, 3 * WIN :, lanes] = lo
                field[pair % 2] = jnp.dot(mixed, w[pair], preferred_element_type=f32)
                rate[pair % 2] = jnp.dot(mixed, d[pair], preferred_element_type=f32)
                for c in range(2):
                    j = pair * 2 + c
                    lanes = slice(c * ATOMS, (c + 1) * ATOMS)
                    row = lambda r: sites[j, r : r + 1, :]
                    taps_z = [spline(row(5)), spline_rate(row(5))]
                    along, slant = z_modes(setup, row(2), taps_z)
                    value = jnp.zeros((16, ATOMS), f32)
                    over_z = jnp.zeros((16, ATOMS), f32)
                    over_y = jnp.zeros((16, ATOMS), f32)
                    for m in range(SLOTS):
                        rows = slice(m * 16, (m + 1) * 16)
                        here = field[pair % 2, rows, lanes]
                        value = value + along[m : m + 1, :] * here
                        over_z = over_z + slant[m : m + 1, :] * here
                        over_y = over_y + along[m : m + 1, :] * rate[pair % 2, rows, lanes]
                    table_x = tap_table(row(0) + 1.0, spline(row(3)), 16)
                    rate_x = tap_table(row(0) + 1.0, spline_rate(row(3)), 16)
                    gather = lambda x: jnp.sum(x, axis=0, keepdims=True)
                    out[j] = jnp.concatenate(
                        [
                            0.5 * gather(table_x * value),
                            -gather(rate_x * value),
                            -gather(table_x * over_y),
                            -gather(table_x * over_z),
                            jnp.zeros((4, ATOMS), f32),
                        ],
                        axis=0,
                    )


def final_kernel(parts, own, energy, force):
    total = parts[0]
    for j in range(1, N_GY):
        total = total + parts[j]
    total = total * own[0]
    energy[0] = total[0:1, :]
    for c in range(3):
        force[c, 0] = total[c + 1 : c + 2, :]


def shape(*dims):
    return jax.ShapeDtypeStruct(dims, f32)


def local(
    positions,
    neighbours,
    live_count,
    stencil_base,
    spline_weight,
    spline_slope,
    embed_scale,
    embed_bias,
    desc_gain,
    fit_in,
    fit_bias,
    fit_hidden,
    fit_bias_two,
    fit_out,
):
    ring = lambda axis, step: [
        (i, (i + step) % lax.axis_size(axis)) for i in range(lax.axis_size(axis))
    ]
    left = lax.ppermute(positions, "gy", ring("gy", 1))
    right = lax.ppermute(positions, "gy", ring("gy", -1))
    column = jnp.concatenate([left, positions, right], axis=0)
    pairs = range(N_GX)
    across = [(i, (i + 1 if i % 2 else i - 1) % N_GX) for i in pairs]
    chip = lax.ppermute(column, "gx", across)
    core = lax.ppermute(column, "gx", [(i, i ^ 1) for i in pairs])

    gx, gy = lax.axis_index("gx"), lax.axis_index("gy")
    device, parity = gy.reshape(1), (gx % 2).reshape(1)
    slot = (gx // 4) * 3 + jnp.arange(3)
    freq_z = gy * 12 + slot % 12
    square_z = jnp.square(freq_z.astype(f32) * WAVE)
    weight_z = jnp.where(freq_z == 0, 1.0, 2.0) / GRID
    quarter = gx % 4
    square = square_z[:, None] + jnp.asarray(SQUARE_Y)[quarter]
    weight = weight_z[:, None] * jnp.asarray(WEIGHT_Y)[quarter]
    middle, gain, device, parity, square, weight = lax.optimization_barrier(
        (column, desc_gain.reshape(DESC, 1), device, parity, square, weight)
    )
    sites, own = pl.pallas_call(
        charge_kernel,
        name="charge",
        out_shape=(shape(N_GY, 8, ATOMS), shape(1, 1, ATOMS)),
        in_specs=[SMEM, SMEM] + vmem(14),
        out_specs=tuple(vmem(2)),
        scratch_shapes=[
            pltpu.VMEM((8, ATOMS), f32),
            pltpu.VMEM((4, EMB_ROWS, ATOMS), f32),
            pltpu.VMEM((DESC, ATOMS), f32),
            pltpu.VMEM((DESC, ATOMS), bf16),
        ],
        compiler_params=PARAMS,
    )(
        live_count,
        parity,
        chip,
        middle,
        core,
        neighbours.reshape(NEIGH, ATOMS),
        stencil_base.reshape(3, 1, 1, ATOMS),
        spline_weight,
        embed_scale.reshape(1, EMB),
        embed_bias.reshape(1, EMB),
        fit_bias.reshape(1, 128),
        fit_bias_two.reshape(1, 128),
        fit_out.reshape(1, 128),
        gain,
        fit_in.T,
        fit_hidden,
    )
    sites = lax.all_to_all(sites, "gy", 0, 0, tiled=True)

    spread = pl.pallas_call(
        forward_kernel,
        name="forward",
        out_shape=shape(N_GX, 36, 128),
        in_specs=[SMEM] + vmem(3),
        out_specs=vmem(1)[0],
        scratch_shapes=[
            pltpu.VMEM((8, GRID, PAIR), bf16),
            pltpu.VMEM((8, GRID, PAIR), bf16),
            pltpu.VMEM((8, 2 * WIN, PAIR), bf16),
            pltpu.VMEM((GRID, SIDE), f32),
        ],
        compiler_params=PARAMS,
    )(device, sites, *Y_IN)
    spread = lax.all_to_all(spread, "gx", 0, 0, tiled=True)

    spread = pl.pallas_call(
        x_kernel,
        name="convolve",
        out_shape=shape(N_GX, 36, 128),
        in_specs=vmem(9),
        out_specs=vmem(1)[0],
        scratch_shapes=[pltpu.VMEM((N_GX * 16, GRID), f32)],
        compiler_params=PARAMS,
    )(square, weight, SQUARE_X, WEIGHT_X, *X_IN, *X_OUT, spread)
    spread = lax.all_to_all(spread, "gx", 0, 0, tiled=True)

    parts = pl.pallas_call(
        inverse_kernel,
        name="inverse",
        out_shape=shape(N_GY, 8, ATOMS),
        in_specs=[SMEM] + vmem(4),
        out_specs=vmem(1)[0],
        scratch_shapes=[
            pltpu.VMEM((2, GRID, SIDE), f32),
            pltpu.VMEM((8, 4 * WIN, PAIR), bf16),
            pltpu.VMEM((8, 4 * WIN, PAIR), bf16),
            pltpu.VMEM((2, GRID, PAIR), f32),
            pltpu.VMEM((2, GRID, PAIR), f32),
        ],
        compiler_params=PARAMS,
    )(device, sites, *Y_OUT, spread)
    parts = lax.all_to_all(parts, "gy", 0, 0, tiled=True)
    energy, force = pl.pallas_call(
        final_kernel,
        name="finish",
        out_shape=(shape(1, 1, ATOMS), shape(3, 1, 1, ATOMS)),
        in_specs=vmem(2),
        out_specs=tuple(vmem(2)),
        compiler_params=PARAMS,
    )(parts, own)
    return energy, force


def solution(mesh):
    placed = (
        P(None, "gx", "gy", None),
        P(None, "gx", "gy", None),
        P("gx", "gy"),
        P(None, "gx", "gy", None),
        P(None, None, "gx", "gy", None),
        P(None, None, "gx", "gy", None),
        P(),
        P(),
        P(),
        P(),
        P(),
        P(),
        P(),
        P(),
    )
    return jax.shard_map(
        local,
        mesh=mesh,
        in_specs=placed,
        out_specs=(P("gx", "gy", None), P(None, "gx", "gy", None)),
        check_vma=False,
    )
```

```python
import math

import jax
import jax.numpy as jnp
import numpy as np
from jax import lax
from jax.experimental import pallas as pl
from jax.experimental.pallas import tpu as pltpu
from jax.sharding import PartitionSpec as P

GRID = 384
AXIS = 16
ATOMS = 128
NEIGH = 32
EMB = 100
EMB_ROWS = 104
DESC = 1600
CX = 12
CY = 24
N_GX = 32
N_GY = 16
SLOTS = 24
LANES = 96
WIN = 64
PAIR = 256

radius_scale = 4.0
screen_width = 0.25
norm_floor = 1e-06
full_turn = 2.0 * math.pi
f32 = jnp.float32
bf16 = jnp.bfloat16


def axis_modes():
    cosines = [(k, 0) for k in range(193)]
    sines = [(k, 1) for k in range(1, 192)]
    modes = [m for odd in (0, 1) for m in cosines + sines if m[0] % 2 == odd]
    return np.array([k for k, _ in modes]), np.array([kind for _, kind in modes])


FREQ, IS_SINE = axis_modes()
WAVE = full_turn / GRID
SIDE = GRID // 2


def mode_table(cells):
    turn = (FREQ[:, None] * cells[None, :] - 96 * IS_SINE[:, None]) % GRID
    return np.cos(full_turn * turn / GRID)


def mode_weight(freq):
    return np.where((freq == 0) | (freq == GRID // 2), 1.0, 2.0) / GRID


def halves(table):
    table = table.astype(np.float32)
    upper = table.astype(jnp.bfloat16)
    lower = (table - upper.astype(np.float32)).astype(jnp.bfloat16)
    return upper, lower


def by_parity(table, stacked):
    out = []
    for part in (table[:SIDE], table[SIDE:]):
        pair = halves(part.T if stacked == "columns" else part)
        out.append(np.concatenate(pair, axis=0) if stacked != "none" else pair)
    return out


CELLS_X = (np.arange(16)[:, None] * CX + np.arange(16)[None, :] - 1).reshape(-1) % GRID
CELLS_Y = (np.arange(4)[:, None] * 2 * CY + np.arange(64)[None, :] - 1).reshape(-1) % GRID
TABLE_X = mode_table(CELLS_X)
TABLE_Y = mode_table(CELLS_Y)
X_IN = by_parity(TABLE_X, "rows")
X_OUT = by_parity(TABLE_X, "columns")
Y_IN = by_parity(TABLE_Y, "columns")
Y_OUT = by_parity(TABLE_Y, "rows")
SQUARE_X = np.broadcast_to(((FREQ * WAVE) ** 2)[:, None], (GRID, 128)).astype(np.float32)
WEIGHT_X = np.broadcast_to(mode_weight(FREQ)[:, None], (GRID, 128)).astype(np.float32)
SQUARE_Y = np.zeros((4, 1, 128), np.float32)
SQUARE_Y[:, 0, :LANES] = ((FREQ * WAVE) ** 2).reshape(4, LANES)
WEIGHT_Y = np.zeros((4, 1, 128), np.float32)
WEIGHT_Y[:, 0, :LANES] = mode_weight(FREQ).reshape(4, LANES)


def split(value):
    upper = value.astype(bf16)
    return upper, (value - upper.astype(f32)).astype(bf16)


def product(left, right, dims=(((1,), (0,)), ((), ()))):
    a, b = left
    c, d = right
    dot = lambda x, y: lax.dot_general(x, y, dims, preferred_element_type=f32)
    return dot(a, c) + (dot(a, d) + dot(b, c))


def vmem(count):
    return [pl.BlockSpec(memory_space=pltpu.VMEM)] * count


SMEM = pl.BlockSpec(memory_space=pltpu.SMEM)
PARAMS = pltpu.CompilerParams(vmem_limit_bytes=48 * 1024 * 1024)


def charge_kernel(
    count, parity, chip, middle, core, listed, base, weight, scale, bias, bias_one, bias_two, read_out,
    gain, fit_in, fit_hidden, sites, own, vectors, mixed, descriptor, normed,
):
    vectors[0:1, 0:EMB] = scale[...]
    vectors[1:2, 0:EMB] = bias[...]
    for k, ref in enumerate((bias_one, bias_two, read_out)):
        vectors[k + 2 : k + 3, :] = ref[...]
    entry = listed[...]
    block = lax.shift_right_logical(entry, 7)
    slot = jnp.bitwise_and(entry, ATOMS - 1)
    picked = [jnp.zeros((NEIGH, ATOMS), f32) for _ in range(3)]
    is_even = jnp.full((1, ATOMS), parity[0], jnp.int32) == 0
    rows_of = (
        lambda r: jnp.where(is_even, chip[r, 0], core[r, 0]),
        lambda r: middle[r, 0],
        lambda r: jnp.where(is_even, core[r, 0], chip[r, 0]),
    )
    for a, rows in enumerate(rows_of):
        for b in range(3):
            here = block == a * 3 + b
            for c, shift in enumerate(((a - 1) * CX, (b - 1) * CY, 0)):
                row = rows(b * 3 + c) + float(shift)
                row = jnp.broadcast_to(row, (NEIGH, ATOMS))
                value = jnp.take_along_axis(row, slot, axis=1)
                picked[c] = jnp.where(here, value, picked[c])
    delta = [picked[c] - middle[3 + c, 0] for c in range(3)]
    radius = jnp.sqrt(delta[0] * delta[0] + delta[1] * delta[1] + delta[2] * delta[2])
    smooth = 1.0 / (1.0 + radius / radius_scale)
    factor = smooth / (radius + radius_scale)
    envelope = [smooth] + [d * factor for d in delta]

    columns = jnp.transpose(vectors[...])
    column = lambda k, lo, hi: jnp.broadcast_to(columns[lo:hi, k : k + 1], (hi - lo, ATOMS))
    for lo, hi in ((0, 32), (32, 64), (64, EMB_ROWS)):
        scale, bias = column(0, lo, hi), column(1, lo, hi)
        total = [jnp.zeros((hi - lo, ATOMS), f32) for _ in range(4)]
        for k in range(NEIGH):
            embed = jnp.tanh(smooth[k : k + 1, :] * scale + bias)
            for c in range(4):
                total[c] = total[c] + embed * envelope[c][k : k + 1, :]
        for c in range(4):
            mixed[c, lo:hi, :] = total[c]
    second_factor = [mixed[c, 0:AXIS, :] for c in range(4)]
    squares = jnp.zeros((AXIS, ATOMS), f32)
    for e in range(EMB):
        value = mixed[0, e : e + 1, :] * second_factor[0]
        for c in range(1, 4):
            value = value + mixed[c, e : e + 1, :] * second_factor[c]
        squares = squares + value * value
        descriptor[e * AXIS : (e + 1) * AXIS, :] = value
    mean = jnp.sum(squares, axis=0, keepdims=True) * (1.0 / DESC)
    scaling = lax.rsqrt(mean + norm_floor)
    for e in range(EMB):
        rows = slice(e * AXIS, (e + 1) * AXIS)
        value = descriptor[rows, :] * scaling * jnp.broadcast_to(gain[rows, :], (AXIS, ATOMS))
        normed[rows, :] = value.astype(bf16)
    first = jnp.tanh(
        lax.dot_general(
            fit_in[...], normed[...], (((0,), (0,)), ((), ())), preferred_element_type=f32
        )
        + column(2, 0, 128)
    )
    second = (
        jnp.tanh(
            jnp.dot(fit_hidden[...], first.astype(bf16), preferred_element_type=f32)
            + column(3, 0, 128)
        )
        + first
    )
    charge = jnp.sum(column(4, 0, 128) * second, axis=0, keepdims=True)
    place = lax.broadcasted_iota(jnp.int32, (1, ATOMS), 1)
    charge = jnp.where(place < count[0, 0], charge, 0.0)
    own[0] = charge
    cell = [base[c, 0].astype(f32) for c in range(3)]
    fraction = [
        weight[c, 1, 0] + 2.0 * weight[c, 2, 0] + 3.0 * weight[c, 3, 0] - 1.0 for c in range(3)
    ]
    record = jnp.concatenate(cell + fraction + [charge, jnp.zeros((1, ATOMS), f32)], axis=0)
    for j in range(N_GY):
        sites[j] = record


def spline(fraction):
    remain = 1.0 - fraction
    square = fraction * fraction
    cube = square * fraction
    return [
        remain * remain * remain * (1.0 / 6.0),
        (3.0 * cube - 6.0 * square + 4.0) * (1.0 / 6.0),
        (-3.0 * cube + 3.0 * square + 3.0 * fraction + 1.0) * (1.0 / 6.0),
        cube * (1.0 / 6.0),
    ]


def spline_rate(fraction):
    remain = 1.0 - fraction
    square = fraction * fraction
    return [
        -0.5 * remain * remain,
        (3.0 * square - 4.0 * fraction) * 0.5,
        (-3.0 * square + 2.0 * fraction + 1.0) * 0.5,
        0.5 * square,
    ]


def tap_table(first, values, rows):
    away = lax.broadcasted_iota(jnp.int32, (rows, ATOMS), 0).astype(f32) - first
    total = jnp.zeros((rows, ATOMS), f32)
    for t, value in enumerate(values):
        total = jnp.where(away == float(t), value, total)
    return total


def cos_sin(step):
    step = step - GRID * jnp.round(step * (1.0 / GRID))
    quarter = jnp.round(step * (1.0 / 96.0))
    angle = (step - 96.0 * quarter) * WAVE
    square = angle * angle
    sine = angle * (
        1.0 + square * (-1.0 / 6 + square * (1.0 / 120 + square * (-1.0 / 5040 + square / 362880)))
    )
    cosine = 1.0 + square * (
        -0.5 + square * (1.0 / 24 + square * (-1.0 / 720 + square * (1.0 / 40320 - square / 3628800)))
    )
    odd = jnp.abs(quarter) == 1.0
    straight = jnp.where(jnp.abs(quarter) == 2.0, -1.0, 1.0)
    turned = jnp.where(odd, quarter, straight)
    cos_value = jnp.where(odd, -sine, cosine) * turned
    sin_value = jnp.where(odd, cosine, sine) * turned
    return cos_value, sin_value


def z_setup(device):
    row = lax.broadcasted_iota(jnp.int32, (SLOTS, ATOMS), 0)
    is_sine = row >= 12
    freq = (device * 12 + jnp.where(is_sine, row - 12, row)).astype(f32)
    phase = jnp.where(is_sine, 96.0, 0.0)
    turns = [cos_sin(freq * float(t)) for t in range(4)]
    return freq, phase, turns


def z_modes(setup, base, lists):
    freq, phase, turns = setup
    cosine, sine = cos_sin(freq * base - phase)
    out = []
    for values in lists:
        along = values[0] + sum(values[t] * turns[t][0] for t in range(1, 4))
        across = sum(values[t] * turns[t][1] for t in range(1, 4))
        out.append(cosine * along - sine * across)
    return out


def pair_table(sites, j, values):
    first = sites[j, 1:2, :] + (1.0 + CY * (j % 2))
    lo, hi = (0, 32) if j % 2 == 0 else (16, 64)
    table = tap_table(first - float(lo), values, hi - lo)
    pieces = [jnp.zeros((lo, ATOMS), f32)] if lo else []
    pieces.append(table)
    if hi < WIN:
        pieces.append(jnp.zeros((WIN - hi, ATOMS), f32))
    return split(jnp.concatenate(pieces, axis=0))


def first_half():
    return lax.broadcasted_iota(jnp.int32, (GRID, 128), 1) < WIN


def forward_kernel(device, sites, even, odd, out, u, w, held):
    setup = z_setup(device[0])
    cells = []
    for pair in range(8):
        for c in range(2):
            j = pair * 2 + c
            lanes = slice(c * ATOMS, (c + 1) * ATOMS)
            row = lambda r: sites[j, r : r + 1, :]
            weight_x = [v * row(6) for v in spline(row(3))]
            table_x = tap_table(row(0) + 1.0, weight_x, 16)
            hi, lo = pair_table(sites, j, spline(row(4)))
            w[pair, 0:WIN, lanes] = hi
            w[pair, WIN:, lanes] = lo
            (along_z,) = z_modes(setup, row(2), [spline(row(5))])
            for m in range(SLOTS):
                spread = along_z[m : m + 1, :] * table_x
                u[pair, m * 16 : (m + 1) * 16, lanes] = spread.astype(bf16)
        dims = (((1,), (1,)), ((), ()))
        both = lax.dot_general(u[pair], w[pair], dims, preferred_element_type=f32)
        cells.append(both + pltpu.roll(both, WIN, 1))
    front = first_half()
    tiles = [jnp.where(front, cells[2 * t], cells[2 * t + 1]) for t in range(4)]
    for parity, table in enumerate((even, odd)):
        sign = 1.0 - 2.0 * parity
        near = jnp.concatenate([tiles[0] + sign * tiles[2], tiles[1] + sign * tiles[3]], axis=1)
        held[...] = product(split(near), (table[0:256, :], table[256:512, :]))
        for side in range(2):
            kq = parity * 2 + side
            block = held[:, side * LANES : (side + 1) * LANES]
            for sg in range(8):
                out[sg * 4 + kq, :, 0:LANES] = block[sg * 48 : sg * 48 + 36, :]
                for p in range(3):
                    out[sg * 4 + kq, 12 * p : 12 * p + 12, LANES:128] = block[
                        sg * 48 + 36 : sg * 48 + 48, 32 * p : 32 * p + 32
                    ]


def x_kernel(square, weight, sx, wx, in_even, in_odd, out_even, out_odd, got, out, held):
    for i in range(N_GX):
        rows = slice(i * 16, (i + 1) * 16)
        for q in range(2):
            held[rows, q * 128 : q * 128 + LANES] = got[i, 16 * q : 16 * q + 16, 0:LANES]
        lane = 2 * 128
        held[i * 16 : i * 16 + 4, lane : lane + LANES] = got[i, 32:36, 0:LANES]
        for p in range(3):
            held[i * 16 + 4 : i * 16 + 16, lane + 32 * p : lane + 32 * p + 32] = got[
                i, 12 * p : 12 * p + 12, LANES:128
            ]
    dot = lambda x, y: jnp.dot(x, y, preferred_element_type=f32)
    near, far = held[0:256, :], held[256:512, :]
    result = []
    for parity, (table_in, table_out) in enumerate(((in_even, out_even), (in_odd, out_odd))):
        hi, lo = split(near + far if parity == 0 else near - far)
        both = dot(table_in[...], hi)
        modes = both[0:SIDE, :] + (both[SIDE:, :] + dot(table_in[0:SIDE, :], lo))
        rows = slice(parity * SIDE, (parity + 1) * SIDE)
        scaled = []
        for q in range(3):
            wave = sx[rows, :] + square[q : q + 1, :]
            safe = jnp.where(wave > 0, wave, 1.0)
            green = 2.0 * full_turn * jnp.exp(-0.5 * screen_width * screen_width * wave) / safe
            green = jnp.where(wave > 0, green, 0.0) * (wx[rows, :] * weight[q : q + 1, :])
            scaled.append(modes[:, q * 128 : (q + 1) * 128] * green)
        hi, lo = split(jnp.concatenate(scaled, axis=1))
        both = dot(table_out[...], hi)
        result.append(both[0:256, :] + (both[256:, :] + dot(table_out[0:256, :], lo)))
    held[0:256, :] = result[0] + result[1]
    held[256:512, :] = result[0] - result[1]
    for i in range(N_GX):
        rows = slice(i * 16, (i + 1) * 16)
        for q in range(2):
            out[i, 16 * q : 16 * q + 16, 0:LANES] = held[rows, q * 128 : q * 128 + LANES]
        lane = 2 * 128
        out[i, 32:36, 0:LANES] = held[i * 16 : i * 16 + 4, lane : lane + LANES]
        for p in range(3):
            out[i, 12 * p : 12 * p + 12, LANES:128] = held[
                i * 16 + 4 : i * 16 + 16, lane + 32 * p : lane + 32 * p + 32
            ]


def inverse_kernel(device, sites, even, odd, got, out, modes, w, d, field, rate):
    setup = z_setup(device[0])
    for kq in range(4):
        part, side = kq // 2, (kq % 2) * LANES
        for sg in range(8):
            row = sg * 48
            modes[part, row : row + 36, side : side + LANES] = got[sg * 4 + kq, :, 0:LANES]
            for p in range(3):
                modes[part, row + 36 : row + 48, side + 32 * p : side + 32 * p + 32] = got[
                    sg * 4 + kq, 12 * p : 12 * p + 12, LANES:128
                ]
    parts = [
        product(split(modes[p]), (table[0:SIDE, :], table[SIDE:, :]))
        for p, table in enumerate((even, odd))
    ]
    halves_y = [parts[0] + parts[1], parts[0] - parts[1]]
    front = first_half()
    for half in range(2):
        for tile in range(2):
            cells = halves_y[half][:, tile * 128 : (tile + 1) * 128]
            turned = pltpu.roll(cells, WIN, 1)
            for p, (near, far) in enumerate(((cells, turned), (turned, cells))):
                pair = half * 4 + tile * 2 + p
                upper = near.astype(bf16).astype(f32)
                lower = far - far.astype(bf16).astype(f32)
                mixed = jnp.where(front, upper, lower).astype(bf16)
                mixed = jnp.concatenate([mixed, mixed], axis=1)
                for c in range(2):
                    j = pair * 2 + c
                    lanes = slice(c * ATOMS, (c + 1) * ATOMS)
                    fraction = sites[j, 4:5, :]
                    for values, ref in ((spline(fraction), w), (spline_rate(fraction), d)):
                        hi, lo = pair_table(sites, j, values)
                        ref[pair, 0:WIN, lanes] = hi
                        ref[pair, WIN : 2 * WIN, lanes] = hi
                        ref[pair, 2 * WIN : 3 * WIN, lanes] = lo
                        ref[pair, 3 * WIN :, lanes] = lo
                field[pair % 2] = jnp.dot(mixed, w[pair], preferred_element_type=f32)
                rate[pair % 2] = jnp.dot(mixed, d[pair], preferred_element_type=f32)
                for c in range(2):
                    j = pair * 2 + c
                    lanes = slice(c * ATOMS, (c + 1) * ATOMS)
                    row = lambda r: sites[j, r : r + 1, :]
                    taps_z = [spline(row(5)), spline_rate(row(5))]
                    along, slant = z_modes(setup, row(2), taps_z)
                    value = jnp.zeros((16, ATOMS), f32)
                    over_z = jnp.zeros((16, ATOMS), f32)
                    over_y = jnp.zeros((16, ATOMS), f32)
                    for m in range(SLOTS):
                        rows = slice(m * 16, (m + 1) * 16)
                        here = field[pair % 2, rows, lanes]
                        value = value + along[m : m + 1, :] * here
                        over_z = over_z + slant[m : m + 1, :] * here
                        over_y = over_y + along[m : m + 1, :] * rate[pair % 2, rows, lanes]
                    table_x = tap_table(row(0) + 1.0, spline(row(3)), 16)
                    rate_x = tap_table(row(0) + 1.0, spline_rate(row(3)), 16)
                    gather = lambda x: jnp.sum(x, axis=0, keepdims=True)
                    out[j] = jnp.concatenate(
                        [
                            0.5 * gather(table_x * value),
                            -gather(rate_x * value),
                            -gather(table_x * over_y),
                            -gather(table_x * over_z),
                            jnp.zeros((4, ATOMS), f32),
                        ],
                        axis=0,
                    )


def final_kernel(parts, own, energy, force):
    total = parts[0]
    for j in range(1, N_GY):
        total = total + parts[j]
    total = total * own[0]
    energy[0] = total[0:1, :]
    for c in range(3):
        force[c, 0] = total[c + 1 : c + 2, :]


def shape(*dims):
    return jax.ShapeDtypeStruct(dims, f32)


def local(
    positions,
    neighbours,
    live_count,
    stencil_base,
    spline_weight,
    spline_slope,
    embed_scale,
    embed_bias,
    desc_gain,
    fit_in,
    fit_bias,
    fit_hidden,
    fit_bias_two,
    fit_out,
):
    ring = lambda axis, step: [
        (i, (i + step) % lax.axis_size(axis)) for i in range(lax.axis_size(axis))
    ]
    left = lax.ppermute(positions, "gy", ring("gy", 1))
    right = lax.ppermute(positions, "gy", ring("gy", -1))
    column = jnp.concatenate([left, positions, right], axis=0)
    pairs = range(N_GX)
    across = [(i, (i + 1 if i % 2 else i - 1) % N_GX) for i in pairs]
    chip = lax.ppermute(column, "gx", across)
    core = lax.ppermute(column, "gx", [(i, i ^ 1) for i in pairs])

    gx, gy = lax.axis_index("gx"), lax.axis_index("gy")
    device, parity = gy.reshape(1), (gx % 2).reshape(1)
    slot = (gx // 4) * 3 + jnp.arange(3)
    freq_z = gy * 12 + slot % 12
    square_z = jnp.square(freq_z.astype(f32) * WAVE)
    weight_z = jnp.where(freq_z == 0, 1.0, 2.0) / GRID
    quarter = gx % 4
    square = square_z[:, None] + jnp.asarray(SQUARE_Y)[quarter]
    weight = weight_z[:, None] * jnp.asarray(WEIGHT_Y)[quarter]
    middle, gain, device, parity, square, weight = lax.optimization_barrier(
        (column, desc_gain.reshape(DESC, 1), device, parity, square, weight)
    )
    sites, own = pl.pallas_call(
        charge_kernel,
        name="charge",
        out_shape=(shape(N_GY, 8, ATOMS), shape(1, 1, ATOMS)),
        in_specs=[SMEM, SMEM] + vmem(14),
        out_specs=tuple(vmem(2)),
        scratch_shapes=[
            pltpu.VMEM((8, ATOMS), f32),
            pltpu.VMEM((4, EMB_ROWS, ATOMS), f32),
            pltpu.VMEM((DESC, ATOMS), f32),
            pltpu.VMEM((DESC, ATOMS), bf16),
        ],
        compiler_params=PARAMS,
    )(
        live_count,
        parity,
        chip,
        middle,
        core,
        neighbours.reshape(NEIGH, ATOMS),
        stencil_base.reshape(3, 1, 1, ATOMS),
        spline_weight,
        embed_scale.reshape(1, EMB),
        embed_bias.reshape(1, EMB),
        fit_bias.reshape(1, 128),
        fit_bias_two.reshape(1, 128),
        fit_out.reshape(1, 128),
        gain,
        fit_in.T,
        fit_hidden,
    )
    sites = lax.all_to_all(sites, "gy", 0, 0, tiled=True)

    spread = pl.pallas_call(
        forward_kernel,
        name="forward",
        out_shape=shape(N_GX, 36, 128),
        in_specs=[SMEM] + vmem(3),
        out_specs=vmem(1)[0],
        scratch_shapes=[
            pltpu.VMEM((8, GRID, PAIR), bf16),
            pltpu.VMEM((8, 2 * WIN, PAIR), bf16),
            pltpu.VMEM((GRID, SIDE), f32),
        ],
        compiler_params=PARAMS,
    )(device, sites, *Y_IN)
    spread = lax.all_to_all(spread, "gx", 0, 0, tiled=True)

    spread = pl.pallas_call(
        x_kernel,
        name="convolve",
        out_shape=shape(N_GX, 36, 128),
        in_specs=vmem(9),
        out_specs=vmem(1)[0],
        scratch_shapes=[pltpu.VMEM((N_GX * 16, GRID), f32)],
        compiler_params=PARAMS,
    )(square, weight, SQUARE_X, WEIGHT_X, *X_IN, *X_OUT, spread)
    spread = lax.all_to_all(spread, "gx", 0, 0, tiled=True)

    parts = pl.pallas_call(
        inverse_kernel,
        name="inverse",
        out_shape=shape(N_GY, 8, ATOMS),
        in_specs=[SMEM] + vmem(4),
        out_specs=vmem(1)[0],
        scratch_shapes=[
            pltpu.VMEM((2, GRID, SIDE), f32),
            pltpu.VMEM((8, 4 * WIN, PAIR), bf16),
            pltpu.VMEM((8, 4 * WIN, PAIR), bf16),
            pltpu.VMEM((2, GRID, PAIR), f32),
            pltpu.VMEM((2, GRID, PAIR), f32),
        ],
        compiler_params=PARAMS,
    )(device, sites, *Y_OUT, spread)
    parts = lax.all_to_all(parts, "gy", 0, 0, tiled=True)
    energy, force = pl.pallas_call(
        final_kernel,
        name="finish",
        out_shape=(shape(1, 1, ATOMS), shape(3, 1, 1, ATOMS)),
        in_specs=vmem(2),
        out_specs=tuple(vmem(2)),
        compiler_params=PARAMS,
    )(parts, own)
    return energy, force


def solution(mesh):
    placed = (
        P(None, "gx", "gy", None),
        P(None, "gx", "gy", None),
        P("gx", "gy"),
        P(None, "gx", "gy", None),
        P(None, None, "gx", "gy", None),
        P(None, None, "gx", "gy", None),
        P(),
        P(),
        P(),
        P(),
        P(),
        P(),
        P(),
        P(),
    )
    return jax.shard_map(
        local,
        mesh=mesh,
        in_specs=placed,
        out_specs=(P("gx", "gy", None), P(None, "gx", "gy", None)),
        check_vma=False,
    )
```
